32 devices in a mesh: period: 4 (over y, x), row: 2 (over core), col: 4 (over z).
Axes of the slice: x: 2, y: 2, z: 4, core: 2. Of those that a mesh axis runs over, the one named last changes fastest.
Arguments:
- primal_start: float32 [512, 512], P(('period', 'row'), 'col'), may hold values from 0 to 1
- dual_start: float32 [512, 256], P(('period', 'col'), 'row'), may hold values from -3 to 3
- objective: float32 [512, 512], P(('period', 'row'), 'col'), may hold values from -28.8 to 28.8
- right_side: float32 [512, 256], P(('period', 'col'), 'row'), may hold values from -28.8 to 28.8
- upper_bound: float32 [512, 512], P(('period', 'row'), 'col'), may hold values from 0.5 to 4
- column_kind: int32 [512, 512], P(('period', 'row'), 'col'), may hold values from 0 to 2
- row_kind: int32 [512, 256], P(('period', 'col'), 'row'), may hold values from 0 to 1
- tile_values: float32 [4, 2, 4, 32, 128, 128], P('period', 'row', 'col'), may hold values from -0.5 to 0.5
- tile_rows: int32 [4, 2, 4, 32], P('period', 'row', 'col'), may hold values from 0 to 127
- tile_cols: int32 [4, 2, 4, 32], P('period', 'row', 'col'), may hold values from 0 to 127
- coupling: float32 [4, 2, 4, 128, 128], P('period', 'row', 'col'), may hold values from -0.5 to 0.5
Outputs:
- primal_final: float32 [512, 512], P(('period', 'row'), 'col')
- dual_final: float32 [512, 256], P(('period', 'col'), 'row')
- primal_weight: float32 [], replicated
The draws below stay inside these ranges and needn't reach their ends.
Inputs may be any that keep to these rules, and one draw needn't show every extreme that they name: `column_kind`: 0: the variable is at least 0; 1: it lies between 0 and its upper_bound; 2: it is free. `row_kind`: 0: the row is an inequality (A x >= right_side, multiplier at least 0); 1: an equality. `tile_rows`: tiles listed twice for the same place add.
All inputs are finite; a program needn't handle non-finite values.
Results may differ from the reference program's by a relative error of at most 0.0001.
Values sent between devices are 32-bit elements; how exact they have to be, the bound alone decides.
No kernel may reach another device: no remote copies, remote signals or barrier semaphores. Data moves between devices by JAX's collectives and lax.ppermute only.
A program may use at most 64 MiB of HBM per device.

```python
import math
import jax
import jax.numpy as jnp
from jax import lax

TILE = 128
CB = 128
RB = 128
NT = 32
ROUNDS = 2
INNER = 2
XROWS = 512
XCOLS = 512
YROWS = 512
YCOLS = 256
N_PERIOD = 4
N_ROW = 2
N_COL = 4


def ramped_field(key, row_count, col_count):
    base_key, rough_key = jax.random.split(key)
    row_ramp = (jnp.arange(row_count, dtype=jnp.float32) / max(row_count - 1, 1))[:, None]
    col_ramp = (jnp.arange(col_count, dtype=jnp.float32) / max(col_count - 1, 1))[None, :]
    rough = jnp.exp(jax.random.uniform(rough_key, (row_count, col_count), jnp.float32, 0.0, math.log(10.0)))
    base = jnp.clip(jax.random.normal(base_key, (row_count, col_count), jnp.float32), -4.0, 4.0)
    ramp = jnp.exp(math.log(3.0) * (row_ramp + col_ramp))
    return 0.08 * base * rough * ramp


def draw_objective(key, part):
    return ramped_field(jax.random.fold_in(key, 11), XROWS, XCOLS)


def draw_right_side(key, part):
    return ramped_field(jax.random.fold_in(key, 23), YROWS, YCOLS)


def set_ends(values, own_key, smallest, top_value):
    spot = [jax.random.randint(jax.random.fold_in(own_key, axis), (), 0, length) for axis, length in enumerate(values.shape)]
    widest = values.shape.index(max(values.shape))
    next_to = spot[:widest] + [(spot[widest] + 1) % values.shape[widest]] + spot[widest + 1:]
    return values.at[tuple(spot)].set(smallest).at[tuple(next_to)].set(top_value)


def block_levels(rng, dims, cuts, low, top_value):
    factor_of = 1.0
    for dim, parts in cuts:
        steps = jax.random.uniform(jax.random.fold_in(jax.random.fold_in(rng, 6), dim), (parts,), jnp.float32, low / len(cuts), top_value / len(cuts))
        factor_of = factor_of * jnp.repeat(jnp.exp(steps), dims[dim] // parts).reshape((-1,) + (1,) * (len(dims) - 1 - dim))
    return factor_of


def centred(key, dims, spread, limit, pieces=(), held_as=jnp.bfloat16):
    level = block_levels(key, dims, pieces, -0.22, 0.18) if pieces else 1.0
    result = jax.random.normal(key, dims, jnp.float32) * spread * level
    return jnp.minimum(jnp.maximum(result, -limit), limit).astype(held_as)


def setup_inputs(seed: int = 0) -> dict:
    arg_keys = jax.random.split(jax.random.key(seed), 12)
    primal_start = jnp.clip(1.0 * jax.random.uniform(arg_keys[0], (XROWS, XCOLS), jnp.float32) ** block_levels(arg_keys[0], (XROWS, XCOLS), ((0, 8), (1, 4)), -0.2, 0.2), 0.0, 1.0)
    dual_start = centred(arg_keys[1], (YROWS, YCOLS), 0.5, 3.0, ((0, 16), (1, 2)), jnp.float32)
    objective = draw_objective(jax.random.fold_in(arg_keys[11], 71), 0)
    right_side = draw_right_side(jax.random.fold_in(arg_keys[11], 71), 0)
    upper_bound = jnp.clip(jnp.exp(math.log(4.0) - 2.0794415 * jax.random.uniform(arg_keys[4], (XROWS, XCOLS), jnp.float32) ** block_levels(arg_keys[4], (XROWS, XCOLS), ((0, 8), (1, 4)), -0.2, 0.2)), 0.5, 4.0)
    column_kind = set_ends(jax.random.randint(arg_keys[5], (XROWS, XCOLS), 0, 3), jax.random.fold_in(arg_keys[5], 1), 0, 2).astype(jnp.int32)
    row_kind = set_ends(jax.random.randint(arg_keys[6], (YROWS, YCOLS), 0, 2), jax.random.fold_in(arg_keys[6], 1), 0, 1).astype(jnp.int32)
    tile_values = centred(arg_keys[7], (N_PERIOD, N_ROW, N_COL, NT, TILE, TILE), TILE ** -0.5, 0.5, ((0, 4), (1, 2), (2, 4)), jnp.float32)
    tile_rows = set_ends(jax.random.randint(arg_keys[8], (N_PERIOD, N_ROW, N_COL, NT), 0, RB), jax.random.fold_in(arg_keys[8], 1), 0, RB - 1).astype(jnp.int32)
    tile_cols = set_ends(jax.random.randint(arg_keys[9], (N_PERIOD, N_ROW, N_COL, NT), 0, CB), jax.random.fold_in(arg_keys[9], 1), 0, CB - 1).astype(jnp.int32)
    coupling = centred(arg_keys[10], (N_PERIOD, N_ROW, N_COL, TILE, TILE), TILE ** -0.5, 0.5, ((0, 4), (1, 2), (2, 4)), jnp.float32)
    return dict(primal_start=primal_start, dual_start=dual_start, objective=objective, right_side=right_side, upper_bound=upper_bound, column_kind=column_kind, row_kind=row_kind, tile_values=tile_values, tile_rows=tile_rows, tile_cols=tile_cols, coupling=coupling)


HIGHEST_MODE = lax.Precision.HIGHEST
STEP_SCALE = 0.15
EPSILON = 1e-06

def apply_forward(primal, tile_values, tile_rows, tile_cols, coupling):
    col_share = CB // N_ROW
    row_share = RB // N_COL
    blocks = primal.reshape(N_PERIOD, CB, N_COL, TILE)
    period_ids = jnp.arange(N_PERIOD, dtype=jnp.int32)[:, None, None, None]
    column_ids = jnp.arange(N_COL, dtype=jnp.int32)[None, None, :, None]
    picked = blocks[period_ids, tile_cols, column_ids]
    products = jnp.einsum('prcnij,prcnj->prcni', tile_values, picked, precision=HIGHEST_MODE)
    row_onehot = (tile_rows[..., None] == jnp.arange(RB, dtype=jnp.int32)).astype(jnp.float32)
    partial_value = jnp.einsum('prcns,prcni->prsi', row_onehot, products, precision=HIGHEST_MODE)
    last_tiles = blocks[:, col_share - 1::col_share, :, :]
    earlier = jnp.concatenate([jnp.zeros((1, N_ROW, N_COL, TILE), jnp.float32), last_tiles[:-1]], axis=0)
    inflow = jnp.einsum('prcij,prcj->prci', coupling, earlier, precision=HIGHEST_MODE)
    partial_value = partial_value.at[:, :, ::row_share, :].add(inflow)
    return partial_value.transpose(0, 2, 1, 3).reshape(N_PERIOD * RB, N_ROW * TILE)

def apply_transpose(dual, tile_values, tile_rows, tile_cols, coupling):
    col_share = CB // N_ROW
    row_share = RB // N_COL
    blocks = dual.reshape(N_PERIOD, RB, N_ROW, TILE)
    period_ids = jnp.arange(N_PERIOD, dtype=jnp.int32)[:, None, None, None]
    row_ids = jnp.arange(N_ROW, dtype=jnp.int32)[None, :, None, None]
    picked = blocks[period_ids, tile_rows, row_ids]
    products = jnp.einsum('prcnij,prcni->prcnj', tile_values, picked, precision=HIGHEST_MODE)
    col_onehot = (tile_cols[..., None] == jnp.arange(CB, dtype=jnp.int32)).astype(jnp.float32)
    partial_value = jnp.einsum('prcnt,prcnj->pctj', col_onehot, products, precision=HIGHEST_MODE)
    first_tiles = blocks[:, ::row_share, :, :]
    outflow = jnp.einsum('prcij,pcri->prcj', coupling, first_tiles, precision=HIGHEST_MODE)
    later = jnp.concatenate([outflow[1:], jnp.zeros((1, N_ROW, N_COL, TILE), jnp.float32)], axis=0)
    partial_value = partial_value.at[:, :, col_share - 1::col_share, :].add(later.transpose(0, 2, 1, 3))
    return partial_value.transpose(0, 2, 1, 3).reshape(N_PERIOD * CB, N_COL * TILE)

def project_primal(values, column_kind, upper_bound):
    lifted = jnp.maximum(values, 0.0)
    boxed = jnp.minimum(lifted, upper_bound)
    return jnp.where(column_kind == 2, values, jnp.where(column_kind == 1, boxed, lifted))

def project_dual(values, row_kind):
    return jnp.where(row_kind == 0, jnp.maximum(values, 0.0), values)

def reference(primal_start, dual_start, objective, right_side, upper_bound, column_kind, row_kind, tile_values, tile_rows, tile_cols, coupling):
    weight = jnp.sqrt((jnp.sum(objective * objective) + EPSILON) / (jnp.sum(right_side * right_side) + EPSILON))
    primal = primal_start
    dual = dual_start
    for round_index in range(ROUNDS):
        primal_step = STEP_SCALE / weight
        dual_step = STEP_SCALE * weight
        primal_begin = primal
        dual_begin = dual
        primal_total = jnp.zeros_like(primal)
        dual_total = jnp.zeros_like(dual)
        for inner_index in range(INNER):
            gradient = objective - apply_transpose(dual, tile_values, tile_rows, tile_cols, coupling)
            primal_next = project_primal(primal - primal_step * gradient, column_kind, upper_bound)
            extrapolated = 2.0 * primal_next - primal
            residual = right_side - apply_forward(extrapolated, tile_values, tile_rows, tile_cols, coupling)
            dual = project_dual(dual + dual_step * residual, row_kind)
            primal = primal_next
            primal_total = primal_total + primal
            dual_total = dual_total + dual
        primal = primal_total / INNER
        dual = dual_total / INNER
        primal_move = jnp.sum((primal - primal_begin) ** 2)
        dual_move = jnp.sum((dual - dual_begin) ** 2)
        weight = jnp.sqrt(weight * jnp.sqrt((primal_move + EPSILON) / (dual_move + EPSILON)))
    return (primal, dual, weight)
```

```python
import functools
import jax
import jax.numpy as jnp
from jax import lax
from jax.experimental import pallas as pl
from jax.experimental.pallas import tpu as pltpu
from jax.sharding import PartitionSpec as P

ROUNDS = 2
INNER = 2
STEP_SCALE = 0.15
EPSILON = 1e-06
F32 = jnp.float32
BF16 = jnp.bfloat16


def up(n, m):
    return -(-n // m) * m


def peer(me, j, n):
    return me ^ j if n & (n - 1) == 0 else lax.rem(me + j, n)


def from_peer(x, axis, j):
    n = lax.axis_size(axis)
    pairs = [((i ^ j) if n & (n - 1) == 0 else (i + j) % n, i) for i in range(n)]
    return lax.ppermute(x, axis, pairs)


def exchange(x, axis):
    return [x] + [from_peer(x, axis, j) for j in range(1, lax.axis_size(axis))]


def period_exchange(x, all_of_them):
    n = lax.axis_size("period")
    if n % 2 == 0 and n > 2:
        even = {i: i ^ 1 for i in range(n)}
        odd = {i: ((i - 1) if i % 2 == 0 else (i + 1)) % n for i in range(n)}
        got = [lax.ppermute(x, "period", [(m[i], i) for i in range(n)]) for m in (even, odd)]
    else:
        got = [lax.ppermute(x, "period", [((i + s) % n, i) for i in range(n)]) for s in (1, n - 1)]
    if all_of_them:
        got += [
            lax.ppermute(x, "period", [((i + s) % n, i) for i in range(n)]) for s in range(2, n - 1)
        ]
    return got


def next_and_previous(first, second, size, me):
    if size % 2 == 0 and size > 2:
        is_even = lax.rem(me, 2) == 0
        return jnp.where(is_even, first, second), jnp.where(is_even, second, first)
    return first, second


def exact_dot(chosen, values):
    head = values.astype(BF16)
    rest = values - head.astype(F32)
    middle = rest.astype(BF16)
    tail = (rest - middle.astype(F32)).astype(BF16)
    dot = functools.partial(jnp.dot, preferred_element_type=F32)
    return dot(chosen, head) + (dot(chosen, middle) + dot(chosen, tail))


def onehot(lists, first, count, height):
    spots = lax.broadcasted_iota(jnp.int32, (height, count), 0).astype(F32)
    return jnp.where(spots == lists[:, first : first + count], 1.0, 0.0).astype(BF16)


def total(x):
    return jnp.sum(jnp.sum(x, axis=0, keepdims=True), axis=1, keepdims=True)


class Sizes:
    def __init__(self, mesh_period, mesh_row, mesh_col, tile, listed, col_share, row_share):
        self.np, self.nr, self.nc = mesh_period, mesh_row, mesh_col
        self.tile, self.nt = tile, listed
        self.cs, self.rs = col_share, row_share
        self.cols, self.rows = col_share * mesh_row, row_share * mesh_col
        self.listed = self.nr * self.nt
        self.products = self.listed + self.nr
        self.blocks = -(-self.products // tile)
        self.zrows = up(self.products + 1, 8)
        self.ghosts = up(self.nr, 8)
        self.xrows = self.cols + self.ghosts
        self.hop = up(2 * self.nr + 2, 8)
        self.hop_first = self.hop + up(4 * self.nr, 8)
        self.group = tile // self.nt
        self.row_lists = -(-self.nc // self.group)
        self.setup = 3 * self.rows + up(self.row_lists + 2, 8)
        self.limit = (self.nr * listed * tile * tile * 4 * 3) // 2 + (10 << 20)


def prepare_kernel(z, dual, rhs, rkind, x, obj, ub, ckind, rlist, clist, zmsg, xmsg):
    rs, cs = z.rs, z.cs
    zmsg[0:rs, :] = dual[...]
    zmsg[rs : 2 * rs, :] = rhs[...]
    zmsg[2 * rs : 3 * rs, :] = jnp.where(rkind[...] == 0, 0.0, -jnp.inf)
    zmsg[3 * rs : 3 * rs + 8, :] = jnp.zeros((8, z.tile), F32)
    zmsg[3 * rs : 3 * rs + 1, :] = rlist[...].astype(F32)
    ones = jnp.ones((1, z.tile), F32)
    zmsg[3 * rs + 1 : 3 * rs + 2, :] = total(obj[...] * obj[...]) * ones
    zmsg[3 * rs + 2 : 3 * rs + 3, :] = total(rhs[...] * rhs[...]) * ones
    kind = ckind[...]
    xmsg[0:cs, :] = x[...]
    xmsg[cs : 2 * cs, :] = obj[...]
    xmsg[2 * cs : 3 * cs, :] = jnp.where(kind == 2, -jnp.inf, 0.0)
    xmsg[3 * cs : 4 * cs, :] = jnp.where(kind == 1, ub[...], jnp.inf)
    xmsg[4 * cs : 4 * cs + 8, :] = jnp.broadcast_to(clist[...].astype(F32), (8, z.tile))


def assemble_kernel(z, *refs):
    slots, out = refs[:-1], refs[-1]
    me = lax.axis_index("col")
    lane = lax.broadcasted_iota(jnp.int32, (1, z.tile), 1)
    base = 3 * z.rows
    out[base:, :] = jnp.zeros((z.setup - base, z.tile), F32)
    sums = jnp.zeros((2, z.tile), F32)
    lists = [jnp.zeros((1, z.tile), F32) for _ in range(z.row_lists)]
    for d, slot in enumerate(slots):
        at = peer(me, d, z.nc) * z.rs
        for part in range(3):
            spot = pl.ds(pl.multiple_of(part * z.rows + at, z.rs), z.rs)
            out[spot, :] = slot[part * z.rs : (part + 1) * z.rs, :]
        mine = lane // z.nt == d % z.group
        q = d // z.group
        lists[q] = jnp.where(mine, slot[3 * z.rs : 3 * z.rs + 1, :], lists[q])
        sums = sums + slot[3 * z.rs + 1 : 3 * z.rs + 3, :]
    for q in range(z.row_lists):
        out[base + q : base + q + 1, :] = lists[q]
    out[base + z.row_lists : base + z.row_lists + 2, :] = sums


def transposed_products(z, y_at, rlists, tiles, links, picked):
    me = lax.axis_index("col")
    picked[...] = jnp.zeros_like(picked)
    for j in range(z.nr):
        for n in range(z.nt):
            k = j * z.nt + n
            picked[k : k + 1, :] = y_at[pl.ds(j * z.rows + rlists[j, n], 1), :]
        k = z.listed + j
        picked[k : k + 1, :] = y_at[pl.ds(j * z.rows + me * z.rs, 1), :]
    turned = [picked[b * z.tile : (b + 1) * z.tile, :].T for b in range(z.blocks)]
    for k in range(z.products):
        if k < z.listed:
            tile = tiles[k // z.nt][k % z.nt]
        else:
            tile = links[k - z.listed][...]
        column = turned[k // z.tile][:, k % z.tile : k % z.tile + 1]
        picked[k : k + 1, :] = jnp.sum(tile * column, axis=0, keepdims=True)


def gradient_part(z, products, clists, g, msg, sums):
    row = lax.axis_index("row")
    full = jnp.zeros((z.cols, z.tile), F32)
    for q in range(-(-z.listed // z.tile)):
        count = min(z.tile, z.listed - q * z.tile)
        lane = lax.broadcasted_iota(jnp.int32, (1, z.tile), 1)
        lists = jnp.zeros((1, z.tile), F32)
        for i in range(count // z.nt):
            lists = jnp.where(lane // z.nt == i, clists[q * z.group + i][0:1, :], lists)
        chosen = onehot(lists, 0, count, z.cols)
        full = full + exact_dot(chosen, products[q * z.tile : q * z.tile + count, :])
    g[0 : z.cols, :] = full
    g[z.cols :, :] = jnp.zeros((z.ghosts, z.tile), F32)
    msg[...] = jnp.zeros_like(msg)
    for j in range(z.nr):
        outflow = products[z.listed + j : z.listed + j + 1, :]
        g[z.cols + j : z.cols + j + 1, :] = outflow
        msg[j : j + 1, :] = outflow
        last = peer(row, j, z.nr) * z.cs + z.cs - 1
        msg[z.nr + j : z.nr + j + 1, :] = g[pl.ds(last, 1), :]
    for i, value in enumerate(sums):
        msg[2 * z.nr + i : 2 * z.nr + i + 1, :] = value


def first_kernel(z, *refs):
    rlists, refs = refs[0], refs[1:]
    shared, refs = refs[: z.nr], refs[z.nr :]
    halves, refs = refs[: z.nr], refs[z.nr :]
    tiles, refs = refs[: z.nr], refs[z.nr :]
    links, refs = refs[: z.nr], refs[z.nr :]
    y, xs, g, msg, picked = refs
    row = lax.axis_index("row")
    for j in range(z.nr):
        y[j * z.rows : (j + 1) * z.rows, :] = shared[j][0 : z.rows, :]
        at = peer(row, j, z.nr) * z.cs
        for part in range(4):
            spot = pl.ds(pl.multiple_of(part * z.xrows + at, 8), z.cs)
            xs[spot, :] = halves[j][part * z.cs : (part + 1) * z.cs, :]
    transposed_products(z, y, rlists, tiles, links, picked)
    base = 3 * z.rows + z.row_lists
    sums = [sum(s[base + i : base + i + 1, :] for s in shared) for i in range(2)]
    gradient_part(
        z, picked, [h.at[4 * z.cs : 4 * z.cs + 8, :] for h in halves], g, msg, sums
    )
    for part in range(4):
        xs[part * z.xrows + z.cols : (part + 1) * z.xrows, :] = jnp.zeros((z.ghosts, z.tile), F32)
        for j in range(z.nr):
            to = z.hop + part * z.nr + j
            msg[to : to + 1, :] = halves[j][(part + 1) * z.cs - 1 : (part + 1) * z.cs, :]


def dual_part(z, w, slots, shared, y_old, y_out):
    me = lax.axis_index("col")
    sigma = STEP_SCALE * w[0:1, :]
    for j in range(z.nr):
        summed = jnp.zeros((z.rows, z.tile), F32)
        for q in range(z.row_lists):
            ds = range(q * z.group, min((q + 1) * z.group, z.nc))
            lists = shared[j][3 * z.rows + q : 3 * z.rows + q + 1, :]
            chosen = onehot(lists, 0, len(ds) * z.nt, z.rows)
            parts = [slots[d][j * z.nt : (j + 1) * z.nt, :] for d in ds]
            summed = summed + exact_dot(chosen, jnp.concatenate(parts, axis=0))
        spot = slice(j * z.rows, (j + 1) * z.rows)
        y_out[spot, :] = summed
        for d in range(z.nc):
            at = pl.ds(j * z.rows + peer(me, d, z.nc) * z.rs, 1)
            y_out[at, :] = y_out[at, :] + slots[d][z.listed + j : z.listed + j + 1, :]
        moved = y_old[spot, :] + sigma * (shared[j][z.rows : 2 * z.rows, :] - y_out[spot, :])
        y_out[spot, :] = jnp.maximum(moved, shared[j][2 * z.rows : 3 * z.rows, :])


def mean_and_move(now, before, begin):
    mean = (now + before) * (1.0 / INNER)
    return mean, total((mean - begin) * (mean - begin))


def dual_kernel(z, ends, *refs):
    rlists, w, refs = refs[0], refs[1], refs[2:]
    slots, refs = refs[: z.nc], refs[z.nc :]
    shared, refs = refs[: z.nr], refs[z.nr :]
    halves, refs = refs[: z.nr], refs[z.nr :]
    tiles, refs = refs[: z.nr], refs[z.nr :]
    links, refs = refs[: z.nr], refs[z.nr :]
    y_old = refs[0]
    y_begin = refs[1] if ends else None
    y_out, g, msg, picked = refs[-4:]
    dual_part(z, w, slots, shared, y_old, y_out)
    sums = []
    if ends:
        mean, move = mean_and_move(y_out[...], y_old[...], y_begin[...])
        y_out[...] = mean
        moved = sum(s[z.products : z.products + 1, :] for s in slots)
        sums = [moved, move * jnp.ones((1, z.tile), F32)]
    transposed_products(z, y_out, rlists, tiles, links, picked)
    gradient_part(
        z, picked, [h.at[4 * z.cs : 4 * z.cs + 8, :] for h in halves], g, msg, sums
    )


def last_kernel(z, *refs):
    w, refs = refs[0], refs[1:]
    slots, refs = refs[: z.nc], refs[z.nc :]
    shared, refs = refs[: z.nr], refs[z.nr :]
    y_old, y_begin, out, msg, y_new = refs
    dual_part(z, w, slots, shared, y_old, y_new)
    mean, move = mean_and_move(y_new[...], y_old[...], y_begin[...])
    y_new[...] = mean
    me = lax.axis_index("col")
    out[...] = y_new[pl.ds(pl.multiple_of(me * z.rs, z.rs), z.rs), :]
    msg[...] = jnp.zeros_like(msg)
    msg[0:1, :] = sum(s[z.products : z.products + 1, :] for s in slots)
    msg[1:2, :] = move * jnp.ones((1, z.tile), F32)


def weight_kernel(z, *refs):
    w, msgs, out = refs[0], refs[1:-1], refs[-1]
    dx = sum(m[0:1, :] for m in msgs)
    dy = sum(m[1:2, :] for m in msgs)
    new = jnp.sqrt(w[0:1, :] * jnp.sqrt((dx + EPSILON) / (dy + EPSILON)))
    out[...] = jnp.broadcast_to(new, out.shape)


def primal_kernel(z, starts, first, ends, last, *refs):
    clists, refs = refs[0], refs[1:]
    w_old, refs = (None, refs) if first else (refs[0], refs[1:])
    g, own, refs = refs[0], refs[1], refs[2:]
    count = (z.np - 1) if starts else 2
    got, refs = refs[:count], refs[count:]
    xs, refs = refs[0], refs[1:]
    x_old, refs = (None, refs) if first else (refs[0], refs[1:])
    x_begin, refs = (refs[0], refs[1:]) if ends else (None, refs)
    tiles, refs = refs[: z.nr], refs[z.nr :]
    links, refs = refs[: z.nr], refs[z.nr :]
    x_out, zmsg, refs = refs[0], refs[1], refs[2:]
    w_out, refs = (refs[0], refs[1:]) if starts else (None, refs)
    xs_out, refs = (refs[0], refs[1:]) if first else (None, refs)
    work, v = refs
    period, row = lax.axis_index("period"), lax.axis_index("row")

    if starts:
        s1 = own[2 * z.nr : 2 * z.nr + 1, :]
        s2 = own[2 * z.nr + 1 : 2 * z.nr + 2, :]
        for m in got:
            s1 = s1 + m[2 * z.nr : 2 * z.nr + 1, :]
            s2 = s2 + m[2 * z.nr + 1 : 2 * z.nr + 2, :]
        ratio = (s1 + EPSILON) / (s2 + EPSILON)
        weight = jnp.sqrt(ratio) if first else jnp.sqrt(w_old[0:1, :] * jnp.sqrt(ratio))
        w_out[...] = jnp.broadcast_to(weight, w_out.shape)
    else:
        weight = w_old[0:1, :]
    tau = STEP_SCALE / weight

    after, before = next_and_previous(got[0][...], got[1][...], z.np, period)
    has_next = period < z.np - 1
    has_previous = period > 0
    work[...] = g[...]
    for j in range(z.nr):
        last_row = pl.ds(peer(row, j, z.nr) * z.cs + z.cs - 1, 1)
        outflow = jnp.where(has_next, after[j : j + 1, :], 0.0)
        work[last_row, :] = work[last_row, :] + outflow
        ghost = slice(z.cols + j, z.cols + j + 1)
        work[ghost, :] = work[ghost, :] + before[z.nr + j : z.nr + j + 1, :]
    if first:
        xs_out[...] = xs[...]
        for part in range(4):
            for j in range(z.nr):
                to = part * z.xrows + z.cols + j
                at = z.hop + part * z.nr + j
                xs_out[to : to + 1, :] = before[at : at + 1, :]
        data = xs_out
        x_now = xs_out[0 : z.xrows, :]
    else:
        data = xs
        x_now = x_old[...]
    obj = data[z.xrows : 2 * z.xrows, :]
    low = data[2 * z.xrows : 3 * z.xrows, :]
    high = data[3 * z.xrows : 4 * z.xrows, :]
    x_new = jnp.minimum(jnp.maximum(x_now - tau * (obj - work[...]), low), high)
    v[...] = 2.0 * x_new - x_now
    v[z.cols :, :] = jnp.where(has_previous, v[z.cols :, :], 0.0)
    move = None
    if ends:
        mean = (x_new + x_now) * (1.0 / INNER)
        moved = mean[0 : z.cols, :] - x_begin[0 : z.cols, :]
        move = total(moved * moved)
        if last:
            work[...] = mean
            x_out[...] = work[pl.ds(pl.multiple_of(row * z.cs, z.cs), z.cs), :]
        else:
            x_out[...] = mean
    else:
        x_out[...] = x_new

    lane = lax.broadcasted_iota(jnp.int32, (z.tile, z.tile), 1)
    for b in range(z.blocks):
        columns = jnp.zeros((z.tile, z.tile), F32)
        for k in range(b * z.tile, min((b + 1) * z.tile, z.products)):
            if k < z.listed:
                tile = tiles[k // z.nt][k % z.nt]
                vector = v[pl.ds(clists[k // z.nt, k % z.nt], 1), :]
            else:
                tile = links[k - z.listed][...]
                vector = v[z.cols + k - z.listed : z.cols + k - z.listed + 1, :]
            column = jnp.sum(tile * vector, axis=1, keepdims=True)
            columns = jnp.where(lane == k % z.tile, column, columns)
        rows = min(z.zrows - b * z.tile, z.tile)
        zmsg[b * z.tile : b * z.tile + rows, :] = columns.T[0:rows, :]
    if ends:
        zmsg[z.products : z.products + 1, :] = move * jnp.ones((1, z.tile), F32)


def call(z, kernel, operands, shapes, scratch=(), smem=0):
    spaces = [pltpu.SMEM] * smem + [pltpu.VMEM] * (len(operands) - smem)
    return pl.pallas_call(
        kernel,
        out_shape=[jax.ShapeDtypeStruct(s, F32) for s in shapes],
        in_specs=[pl.BlockSpec(memory_space=s) for s in spaces],
        out_specs=[pl.BlockSpec(memory_space=pltpu.VMEM) for _ in shapes],
        scratch_shapes=[pltpu.VMEM(s, F32) for s in scratch],
        compiler_params=pltpu.CompilerParams(vmem_limit_bytes=z.limit),
    )(*operands)


def per_device(
    primal_start,
    dual_start,
    objective,
    right_side,
    upper_bound,
    column_kind,
    row_kind,
    tile_values,
    tile_rows,
    tile_cols,
    coupling,
):
    tile = tile_values.shape[-1]
    listed = tile_values.shape[3]
    z = Sizes(
        lax.axis_size("period"),
        lax.axis_size("row"),
        lax.axis_size("col"),
        tile,
        listed,
        primal_start.shape[0],
        dual_start.shape[0],
    )
    part = functools.partial
    line = lambda rows: (rows, tile)
    row_list = tile_rows.reshape(1, listed)
    col_list = tile_cols.reshape(1, listed)
    tiles = exchange(tile_values.reshape(listed, tile, tile), "row")
    links = exchange(coupling.reshape(tile, tile), "row")
    both = jnp.concatenate([row_list, col_list], axis=0)
    lists = exchange(both, "row")
    rlists = jnp.concatenate([b[0:1] for b in lists], axis=0)
    clists = jnp.concatenate([b[1:2] for b in lists], axis=0)

    zmsg, xmsg = call(
        z,
        part(prepare_kernel, z),
        (
            dual_start,
            right_side,
            row_kind,
            primal_start,
            objective,
            upper_bound,
            column_kind,
            jnp.tile(row_list, (1, z.group)),
            jnp.tile(col_list, (1, z.group)),
        ),
        [line(3 * z.rs + 8), line(4 * z.cs + 8)],
    )
    slots = exchange(zmsg, "col")
    halves = exchange(xmsg, "row")
    (gathered,) = call(z, part(assemble_kernel, z), slots, [line(z.setup)])
    shared = exchange(gathered, "row")

    picked = line(z.blocks * tile)
    y, xs, g, msg = call(
        z,
        part(first_kernel, z),
        (rlists, *shared, *halves, *tiles, *links),
        [line(z.nr * z.rows), line(4 * z.xrows), line(z.xrows), line(z.hop_first)],
        [picked],
        smem=1,
    )
    x = None
    weight = None
    y_begin, x_begin = y, None
    for step in range(ROUNDS * INNER):
        starts = step % INNER == 0
        ends = step % INNER == INNER - 1
        first, last = step == 0, step == ROUNDS * INNER - 1
        got = period_exchange(msg, starts)
        operands = [clists] + ([] if first else [weight]) + [g, msg, *got, xs]
        operands += ([] if first else [x]) + ([x_begin] if ends else []) + [*tiles, *links]
        shapes = [line(z.cs if last else z.xrows), line(z.zrows)]
        shapes += ([line(8)] if starts else []) + ([line(4 * z.xrows)] if first else [])
        outs = call(
            z,
            part(primal_kernel, z, starts, first, ends, last),
            operands,
            shapes,
            [line(z.xrows), line(z.xrows)],
            smem=1,
        )
        x_next, zmsg = outs[:2]
        if starts:
            weight = outs[2]
        if first:
            xs = outs[3]
            x = xs[0 : z.xrows]
        if starts:
            x_begin = x
        x = x_next
        slots = exchange(zmsg, "col")
        if last:
            break
        operands = [rlists, weight, *slots, *shared, *halves, *tiles, *links, y]
        y_next, g, msg = call(
            z,
            part(dual_kernel, z, ends),
            operands + ([y_begin] if ends else []),
            [line(z.nr * z.rows), line(z.xrows), line(z.hop)],
            [picked],
            smem=1,
        )
        y = y_next
        if ends:
            y_begin = y
    dual, sums = call(
        z,
        part(last_kernel, z),
        (weight, *slots, *shared, y, y_begin),
        [line(z.rs), line(8)],
        [line(z.nr * z.rows)],
    )
    (final,) = call(
        z,
        part(weight_kernel, z),
        (weight, sums, *period_exchange(sums, True)),
        [line(8)],
    )
    return (x, dual, final[0, 0])


def solution(mesh):
    in_specs = (
        P(("period", "row"), "col"),
        P(("period", "col"), "row"),
        P(("period", "row"), "col"),
        P(("period", "col"), "row"),
        P(("period", "row"), "col"),
        P(("period", "row"), "col"),
        P(("period", "col"), "row"),
        P("period", "row", "col", None, None, None),
        P("period", "row", "col", None),
        P("period", "row", "col", None),
        P("period", "row", "col", None, None),
    )
    out_specs = (P(("period", "row"), "col"), P(("period", "col"), "row"), P())
    return jax.shard_map(
        per_device, mesh=mesh, in_specs=in_specs, out_specs=out_specs, check_vma=False
    )
```

```python
import functools
import jax
import jax.numpy as jnp
from jax import lax
from jax.experimental import pallas as pl
from jax.experimental.pallas import tpu as pltpu
from jax.sharding import PartitionSpec as P

ROUNDS = 2
INNER = 2
STEP_SCALE = 0.15
EPSILON = 1e-06
F32 = jnp.float32
BF16 = jnp.bfloat16
FETCH = 51 << 20
AWAY = 59 << 20
FETCHES = 8


def up(n, m):
    return -(-n // m) * m


def peer(me, j, n):
    return me ^ j if n & (n - 1) == 0 else lax.rem(me + j, n)


def from_peer(x, axis, j):
    n = lax.axis_size(axis)
    pairs = [((i ^ j) if n & (n - 1) == 0 else (i + j) % n, i) for i in range(n)]
    return lax.ppermute(x, axis, pairs)


def exchange(x, axis):
    return [x] + [from_peer(x, axis, j) for j in range(1, lax.axis_size(axis))]


def period_exchange(x, all_of_them):
    n = lax.axis_size("period")
    if n % 2 == 0 and n > 2:
        even = {i: i ^ 1 for i in range(n)}
        odd = {i: ((i - 1) if i % 2 == 0 else (i + 1)) % n for i in range(n)}
        got = [lax.ppermute(x, "period", [(m[i], i) for i in range(n)]) for m in (even, odd)]
    else:
        got = [lax.ppermute(x, "period", [((i + s) % n, i) for i in range(n)]) for s in (1, n - 1)]
    if all_of_them:
        got += [
            lax.ppermute(x, "period", [((i + s) % n, i) for i in range(n)]) for s in range(2, n - 1)
        ]
    return got


def next_and_previous(first, second, size, me):
    if size % 2 == 0 and size > 2:
        is_even = lax.rem(me, 2) == 0
        return jnp.where(is_even, first, second), jnp.where(is_even, second, first)
    return first, second


def onehot(lists, first, count, height):
    spots = lax.broadcasted_iota(jnp.int32, (height, count), 0).astype(F32)
    return jnp.where(spots == lists[:, first : first + count], 1.0, 0.0).astype(BF16)


def total(x):
    return jnp.sum(jnp.sum(x, axis=0, keepdims=True), axis=1, keepdims=True)


class Sizes:
    def __init__(self, mesh_period, mesh_row, mesh_col, tile, listed, col_share, row_share):
        self.np, self.nr, self.nc = mesh_period, mesh_row, mesh_col
        self.tile, self.nt = tile, listed
        self.cs, self.rs = col_share, row_share
        self.cols, self.rows = col_share * mesh_row, row_share * mesh_col
        self.listed = self.nr * self.nt
        self.products = self.listed + self.nr
        self.blocks = -(-self.products // tile)
        self.zrows = up(self.products + 1, 8)
        self.ghosts = up(self.nr, 8)
        self.xrows = self.cols + self.ghosts
        self.hop = up(2 * self.nr + 2, 8)
        self.hop_first = self.hop + up(4 * self.nr, 8)
        self.group = tile // self.nt
        self.row_lists = -(-self.nc // self.group)
        self.setup = 3 * self.rows + up(self.row_lists + 2, 8)
        self.link = 4 * col_share + 8
        self.limit = (self.nr * listed * tile * tile * 4 * 3) // 2 + (10 << 20)


def copies(pairs, sems):
    started = [pltpu.make_async_copy(src, dst, sems.at[i]) for i, (src, dst) in enumerate(pairs)]
    for copy in started:
        copy.start()
    for copy in started:
        copy.wait()


def dual_message_kernel(z, dual_at, rhs_at, rkind_at, obj_at, rlist_at, zmsg, rkind, obj, rlist, sems):
    rs = z.rs
    copies(
        [
            (dual_at, zmsg.at[0:rs, :]),
            (rhs_at, zmsg.at[rs : 2 * rs, :]),
            (rkind_at, rkind),
            (obj_at, obj),
            (rlist_at, rlist),
        ],
        sems,
    )
    rhs = zmsg[rs : 2 * rs, :]
    zmsg[2 * rs : 3 * rs, :] = jnp.where(rkind[...] == 0, 0.0, -jnp.inf)
    zmsg[3 * rs : 3 * rs + 8, :] = jnp.zeros((8, z.tile), F32)
    zmsg[3 * rs : 3 * rs + 1, 0 : z.nt] = rlist[...].astype(F32)
    ones = jnp.ones((1, z.tile), F32)
    zmsg[3 * rs + 1 : 3 * rs + 2, :] = total(obj[...] * obj[...]) * ones
    zmsg[3 * rs + 2 : 3 * rs + 3, :] = total(rhs * rhs) * ones


def primal_message_kernel(
    z, x_at, obj_at, ub_at, ckind_at, clist_at, link_at, xmsg, ub, ckind, clist, sems
):
    cs = z.cs
    copies(
        [
            (x_at, xmsg.at[0:cs, :]),
            (obj_at, xmsg.at[cs : 2 * cs, :]),
            (ub_at, ub),
            (ckind_at, ckind),
            (clist_at, clist),
            (link_at, xmsg.at[z.link : z.link + z.tile, :]),
        ],
        sems,
    )
    kind = ckind[...]
    xmsg[2 * cs : 3 * cs, :] = jnp.where(kind == 2, -jnp.inf, 0.0)
    xmsg[3 * cs : 4 * cs, :] = jnp.where(kind == 1, ub[...], jnp.inf)
    xmsg[4 * cs : 4 * cs + 8, :] = jnp.zeros((8, z.tile), F32)
    xmsg[4 * cs : 4 * cs + 1, 0 : z.nt] = clist[...].astype(F32)


def fetch_kernel(z, tiles_at, tiles, token, sems):
    step = max(z.nt // FETCHES, 1)
    cuts = range(0, z.nt, step)
    copies([(tiles_at.at[i : i + step], tiles.at[i : i + step]) for i in cuts], sems)
    token[...] = jnp.zeros_like(token)


def put_list(z, lists, rows, i):
    lane = lax.broadcasted_iota(jnp.int32, (8, z.tile), 1)
    moved = pltpu.roll(rows, i * z.nt, 1) if i else rows
    return jnp.where(lane // z.nt == i, moved, lists)


def assemble_kernel(z, *refs):
    slots, out = refs[1:-1], refs[-1]
    me = lax.axis_index("col")
    base = 3 * z.rows
    out[base:, :] = jnp.zeros((z.setup - base, z.tile), F32)
    sums = jnp.zeros((2, z.tile), F32)
    lists = [jnp.zeros((8, z.tile), F32) for _ in range(z.row_lists)]
    for d, slot in enumerate(slots):
        at = peer(me, d, z.nc) * z.rs
        for part in range(3):
            spot = pl.ds(pl.multiple_of(part * z.rows + at, z.rs), z.rs)
            out[spot, :] = slot[part * z.rs : (part + 1) * z.rs, :]
        q = d // z.group
        lists[q] = put_list(z, lists[q], slot[3 * z.rs : 3 * z.rs + 8, :], d % z.group)
        sums = sums + slot[3 * z.rs + 1 : 3 * z.rs + 3, :]
    for q in range(z.row_lists):
        out[base + q : base + q + 1, :] = lists[q][0:1, :]
    out[base + z.row_lists : base + z.row_lists + 2, :] = sums


def three_parts(values):
    head = values.astype(BF16)
    rest = values - head.astype(F32)
    middle = rest.astype(BF16)
    return head, middle, (rest - middle.astype(F32)).astype(BF16)


def exact_dot(chosen, values):
    head, middle, tail = three_parts(values)
    dot = functools.partial(jnp.dot, preferred_element_type=F32)
    return dot(chosen, head) + (dot(chosen, middle) + dot(chosen, tail))


def exact_turned_dot(left, right):
    dot = lambda a, b: lax.dot_general(
        a, b, (((0,), (0,)), ((), ())), preferred_element_type=F32
    )
    if left.dtype == BF16:
        head, middle, tail = three_parts(right)
        return dot(left, head) + (dot(left, middle) + dot(left, tail))
    head, middle, tail = three_parts(left)
    return dot(head, right) + (dot(middle, right) + dot(tail, right))


def transposed_products(z, y_at, shared, tiles, links, products):
    me = lax.axis_index("col")
    for j in range(z.nr):
        chosen = onehot(shared[j][3 * z.rows : 3 * z.rows + 1, :], 0, z.nt, z.rows)
        columns = exact_turned_dot(y_at[j * z.rows : (j + 1) * z.rows, :], chosen)
        first = y_at[pl.ds(j * z.rows + me * z.rs, 1), :]
        coupled = jnp.broadcast_to(first, (8, z.tile)).T
        for n in range(z.nt):
            k = j * z.nt + n
            column = columns[:, n : n + 1]
            products[k : k + 1, :] = jnp.sum(tiles[j][n] * column, axis=0, keepdims=True)
        k = z.listed + j
        link = links[j][z.link : z.link + z.tile, :]
        products[k : k + 1, :] = jnp.sum(link * coupled[:, 0:1], axis=0, keepdims=True)


def column_lists(z, halves, q):
    lists = jnp.zeros((8, z.tile), F32)
    for i in range(min(z.group, z.nr - q * z.group)):
        at = 4 * z.cs
        lists = put_list(z, lists, halves[q * z.group + i][at : at + 8, :], i)
    return lists[0:1, :]


def gradient_part(z, products, halves, g, msg, sums):
    row = lax.axis_index("row")
    full = jnp.zeros((z.cols, z.tile), F32)
    for q in range(-(-z.listed // z.tile)):
        count = min(z.tile, z.listed - q * z.tile)
        chosen = onehot(column_lists(z, halves, q), 0, count, z.cols)
        full = full + exact_dot(chosen, products[q * z.tile : q * z.tile + count, :])
    g[0 : z.cols, :] = full
    g[z.cols :, :] = jnp.zeros((z.ghosts, z.tile), F32)
    msg[...] = jnp.zeros_like(msg)
    for j in range(z.nr):
        outflow = products[z.listed + j : z.listed + j + 1, :]
        g[z.cols + j : z.cols + j + 1, :] = outflow
        msg[j : j + 1, :] = outflow
        last = peer(row, j, z.nr) * z.cs + z.cs - 1
        msg[z.nr + j : z.nr + j + 1, :] = g[pl.ds(last, 1), :]
    for i, value in enumerate(sums):
        msg[2 * z.nr + i : 2 * z.nr + i + 1, :] = value


def first_kernel(z, *refs):
    shared, refs = refs[: z.nr], refs[z.nr :]
    halves, refs = refs[: z.nr], refs[z.nr :]
    tiles, refs = refs[: z.nr], refs[z.nr :]
    y, xs, g, msg, products = refs
    row = lax.axis_index("row")
    for j in range(z.nr):
        y[j * z.rows : (j + 1) * z.rows, :] = shared[j][0 : z.rows, :]
        at = peer(row, j, z.nr) * z.cs
        for part in range(4):
            spot = pl.ds(pl.multiple_of(part * z.xrows + at, 8), z.cs)
            xs[spot, :] = halves[j][part * z.cs : (part + 1) * z.cs, :]
    transposed_products(z, y, shared, tiles, halves, products)
    base = 3 * z.rows + z.row_lists
    sums = [sum(s[base + i : base + i + 1, :] for s in shared) for i in range(2)]
    gradient_part(z, products, halves, g, msg, sums)
    for part in range(4):
        xs[part * z.xrows + z.cols : (part + 1) * z.xrows, :] = jnp.zeros((z.ghosts, z.tile), F32)
        for j in range(z.nr):
            to = z.hop + part * z.nr + j
            msg[to : to + 1, :] = halves[j][(part + 1) * z.cs - 1 : (part + 1) * z.cs, :]


def dual_part(z, w, slots, shared, y_old, y_out):
    me = lax.axis_index("col")
    sigma = STEP_SCALE * w[0:1, :]
    for j in range(z.nr):
        summed = jnp.zeros((z.rows, z.tile), F32)
        for q in range(z.row_lists):
            ds = range(q * z.group, min((q + 1) * z.group, z.nc))
            lists = shared[j][3 * z.rows + q : 3 * z.rows + q + 1, :]
            chosen = onehot(lists, 0, len(ds) * z.nt, z.rows)
            parts = [slots[d][j * z.nt : (j + 1) * z.nt, :] for d in ds]
            summed = summed + exact_dot(chosen, jnp.concatenate(parts, axis=0))
        spot = slice(j * z.rows, (j + 1) * z.rows)
        y_out[spot, :] = summed
        for d in range(z.nc):
            at = pl.ds(j * z.rows + peer(me, d, z.nc) * z.rs, 1)
            y_out[at, :] = y_out[at, :] + slots[d][z.listed + j : z.listed + j + 1, :]
        moved = y_old[spot, :] + sigma * (shared[j][z.rows : 2 * z.rows, :] - y_out[spot, :])
        y_out[spot, :] = jnp.maximum(moved, shared[j][2 * z.rows : 3 * z.rows, :])


def mean_and_move(now, before, begin):
    mean = (now + before) * (1.0 / INNER)
    return mean, total((mean - begin) * (mean - begin))


def dual_kernel(z, ends, *refs):
    w, refs = refs[0], refs[1:]
    slots, refs = refs[: z.nc], refs[z.nc :]
    shared, refs = refs[: z.nr], refs[z.nr :]
    halves, refs = refs[: z.nr], refs[z.nr :]
    tiles, refs = refs[: z.nr], refs[z.nr :]
    y_old = refs[0]
    y_begin = refs[1] if ends else None
    y_out, g, msg, products = refs[-4:]
    dual_part(z, w, slots, shared, y_old, y_out)
    sums = []
    if ends:
        mean, move = mean_and_move(y_out[...], y_old[...], y_begin[...])
        y_out[...] = mean
        moved = sum(s[z.products : z.products + 1, :] for s in slots)
        sums = [moved, move * jnp.ones((1, z.tile), F32)]
    transposed_products(z, y_out, shared, tiles, halves, products)
    gradient_part(z, products, halves, g, msg, sums)


def last_kernel(z, *refs):
    w, refs = refs[0], refs[1:]
    slots, refs = refs[: z.nc], refs[z.nc :]
    shared, refs = refs[: z.nr], refs[z.nr :]
    y_old, y_begin, out, msg, y_new = refs
    dual_part(z, w, slots, shared, y_old, y_new)
    mean, move = mean_and_move(y_new[...], y_old[...], y_begin[...])
    y_new[...] = mean
    me = lax.axis_index("col")
    out[...] = y_new[pl.ds(pl.multiple_of(me * z.rs, z.rs), z.rs), :]
    msg[...] = jnp.zeros_like(msg)
    msg[0:1, :] = sum(s[z.products : z.products + 1, :] for s in slots)
    msg[1:2, :] = move * jnp.ones((1, z.tile), F32)


def weight_kernel(z, *refs):
    w, msgs, out = refs[0], refs[1:-1], refs[-1]
    dx = sum(m[0:1, :] for m in msgs)
    dy = sum(m[1:2, :] for m in msgs)
    new = jnp.sqrt(w[0:1, :] * jnp.sqrt((dx + EPSILON) / (dy + EPSILON)))
    out[0] = new[0, 0]


def primal_kernel(z, starts, first, ends, last, *refs):
    w_old, refs = (None, refs) if first else (refs[0], refs[1:])
    g, own, refs = refs[0], refs[1], refs[2:]
    count = (z.np - 1) if starts else 2
    got, refs = refs[:count], refs[count:]
    xs, refs = refs[0], refs[1:]
    x_old, refs = (None, refs) if first else (refs[0], refs[1:])
    x_begin, refs = (refs[0], refs[1:]) if ends else (None, refs)
    halves, refs = refs[: z.nr], refs[z.nr :]
    tiles, refs = refs[: z.nr], refs[z.nr :]
    x_out, zmsg, refs = refs[0], refs[1], refs[2:]
    w_out, refs = (refs[0], refs[1:]) if starts else (None, refs)
    xs_out, refs = (refs[0], refs[1:]) if first else (None, refs)
    work, v, vectors = refs
    period, row = lax.axis_index("period"), lax.axis_index("row")

    if starts:
        s1 = own[2 * z.nr : 2 * z.nr + 1, :]
        s2 = own[2 * z.nr + 1 : 2 * z.nr + 2, :]
        for m in got:
            s1 = s1 + m[2 * z.nr : 2 * z.nr + 1, :]
            s2 = s2 + m[2 * z.nr + 1 : 2 * z.nr + 2, :]
        ratio = (s1 + EPSILON) / (s2 + EPSILON)
        weight = jnp.sqrt(ratio) if first else jnp.sqrt(w_old[0:1, :] * jnp.sqrt(ratio))
        w_out[...] = jnp.broadcast_to(weight, w_out.shape)
    else:
        weight = w_old[0:1, :]
    tau = STEP_SCALE / weight

    after, before = next_and_previous(got[0][...], got[1][...], z.np, period)
    has_next = period < z.np - 1
    has_previous = period > 0
    work[...] = g[...]
    for j in range(z.nr):
        last_row = pl.ds(peer(row, j, z.nr) * z.cs + z.cs - 1, 1)
        outflow = jnp.where(has_next, after[j : j + 1, :], 0.0)
        work[last_row, :] = work[last_row, :] + outflow
        ghost = slice(z.cols + j, z.cols + j + 1)
        work[ghost, :] = work[ghost, :] + before[z.nr + j : z.nr + j + 1, :]
    if first:
        xs_out[...] = xs[...]
        for part in range(4):
            for j in range(z.nr):
                to = part * z.xrows + z.cols + j
                at = z.hop + part * z.nr + j
                xs_out[to : to + 1, :] = before[at : at + 1, :]
        data = xs_out
        x_now = xs_out[0 : z.xrows, :]
    else:
        data = xs
        x_now = x_old[...]
    obj = data[z.xrows : 2 * z.xrows, :]
    low = data[2 * z.xrows : 3 * z.xrows, :]
    high = data[3 * z.xrows : 4 * z.xrows, :]
    x_new = jnp.minimum(jnp.maximum(x_now - tau * (obj - work[...]), low), high)
    v[...] = 2.0 * x_new - x_now
    v[z.cols :, :] = jnp.where(has_previous, v[z.cols :, :], 0.0)
    move = None
    if ends:
        mean = (x_new + x_now) * (1.0 / INNER)
        moved = mean[0 : z.cols, :] - x_begin[0 : z.cols, :]
        move = total(moved * moved)
        if last:
            work[...] = mean
            x_out[...] = work[pl.ds(pl.multiple_of(row * z.cs, z.cs), z.cs), :]
        else:
            x_out[...] = mean
    else:
        x_out[...] = x_new

    for q in range(-(-z.listed // z.tile)):
        count = min(z.tile, z.listed - q * z.tile)
        chosen = onehot(column_lists(z, halves, q), 0, count, z.cols)
        vectors[q * z.tile : q * z.tile + count, :] = exact_turned_dot(chosen, v[0 : z.cols, :])
    lane = lax.broadcasted_iota(jnp.int32, (z.tile, z.tile), 1)
    for b in range(z.blocks):
        columns = jnp.zeros((z.tile, z.tile), F32)
        for k in range(b * z.tile, min((b + 1) * z.tile, z.products)):
            if k < z.listed:
                tile = tiles[k // z.nt][k % z.nt]
                vector = vectors[k : k + 1, :]
            else:
                tile = halves[k - z.listed][z.link : z.link + z.tile, :]
                vector = v[z.cols + k - z.listed : z.cols + k - z.listed + 1, :]
            column = jnp.sum(tile * vector, axis=1, keepdims=True)
            columns = jnp.where(lane == k % z.tile, column, columns)
        rows = min(z.zrows - b * z.tile, z.tile)
        zmsg[b * z.tile : b * z.tile + rows, :] = columns.T[0:rows, :]
    if ends:
        zmsg[z.products : z.products + 1, :] = move * jnp.ones((1, z.tile), F32)


def call(z, kernel, operands, shapes, scratch=(), away=0, sems=0, scalar=False, limit=None):
    spaces = [pl.ANY] * away + [pltpu.VMEM] * (len(operands) - away)
    kinds = [s if isinstance(s, tuple) and isinstance(s[0], tuple) else (s, F32) for s in scratch]
    return pl.pallas_call(
        kernel,
        out_shape=[jax.ShapeDtypeStruct(s, F32) for s in shapes],
        in_specs=[pl.BlockSpec(memory_space=s) for s in spaces],
        out_specs=[
            pl.BlockSpec(memory_space=pltpu.SMEM if scalar else pltpu.VMEM) for _ in shapes
        ],
        scratch_shapes=[pltpu.VMEM(s, kind) for s, kind in kinds]
        + ([pltpu.SemaphoreType.DMA((sems,))] if sems else []),
        compiler_params=pltpu.CompilerParams(vmem_limit_bytes=limit or z.limit),
    )(*operands)


def per_device(
    primal_start,
    dual_start,
    objective,
    right_side,
    upper_bound,
    column_kind,
    row_kind,
    tile_values,
    tile_rows,
    tile_cols,
    coupling,
):
    tile = tile_values.shape[-1]
    listed = tile_values.shape[3]
    z = Sizes(
        lax.axis_size("period"),
        lax.axis_size("row"),
        lax.axis_size("col"),
        tile,
        listed,
        primal_start.shape[0],
        dual_start.shape[0],
    )
    part = functools.partial
    line = lambda rows: (rows, tile)
    row_list = tile_rows.reshape(1, listed)
    col_list = tile_cols.reshape(1, listed)
    tiles_away = tile_values.reshape(listed, tile, tile)
    tiles = exchange(tiles_away, "row")
    (zmsg,) = call(
        z,
        part(dual_message_kernel, z),
        (dual_start, right_side, row_kind, objective, row_list),
        [line(3 * z.rs + 8)],
        [(line(z.rs), jnp.int32), line(z.cs), ((1, listed), jnp.int32)],
        away=5,
        sems=5,
        limit=AWAY,
    )
    (xmsg,) = call(
        z,
        part(primal_message_kernel, z),
        (
            primal_start,
            objective,
            upper_bound,
            column_kind,
            col_list,
            coupling.reshape(tile, tile),
        ),
        [line(z.link + tile)],
        [line(z.cs), (line(z.cs), jnp.int32), ((1, listed), jnp.int32)],
        away=6,
        sems=6,
        limit=AWAY,
    )
    tiles[0], token = call(
        z,
        part(fetch_kernel, z),
        (tiles_away,),
        [(listed, tile, tile), line(8)],
        away=1,
        sems=FETCHES,
        limit=FETCH,
    )
    slots = exchange(zmsg, "col")
    halves = exchange(xmsg, "row")
    (gathered,) = call(z, part(assemble_kernel, z), [token] + slots, [line(z.setup)])
    shared = exchange(gathered, "row")

    products = line(up(z.products, 8))
    y, xs, g, msg = call(
        z,
        part(first_kernel, z),
        (*shared, *halves, *tiles),
        [line(z.nr * z.rows), line(4 * z.xrows), line(z.xrows), line(z.hop_first)],
        [products],
    )
    x = None
    weight = None
    y_begin, x_begin = y, None
    for step in range(ROUNDS * INNER):
        starts = step % INNER == 0
        ends = step % INNER == INNER - 1
        first, last = step == 0, step == ROUNDS * INNER - 1
        got = period_exchange(msg, starts)
        operands = ([] if first else [weight]) + [g, msg, *got, xs]
        operands += ([] if first else [x]) + ([x_begin] if ends else []) + [*halves, *tiles]
        shapes = [line(z.cs if last else z.xrows), line(z.zrows)]
        shapes += ([line(8)] if starts else []) + ([line(4 * z.xrows)] if first else [])
        outs = call(
            z,
            part(primal_kernel, z, starts, first, ends, last),
            operands,
            shapes,
            [line(z.xrows), line(z.xrows), line(up(z.listed, 8))],
        )
        x_next, zmsg = outs[:2]
        if starts:
            weight = outs[2]
        if first:
            xs = outs[3]
            x = xs[0 : z.xrows]
        if starts:
            x_begin = x
        x = x_next
        slots = exchange(zmsg, "col")
        if last:
            break
        operands = [weight, *slots, *shared, *halves, *tiles, y]
        y_next, g, msg = call(
            z,
            part(dual_kernel, z, ends),
            operands + ([y_begin] if ends else []),
            [line(z.nr * z.rows), line(z.xrows), line(z.hop)],
            [products],
        )
        y = y_next
        if ends:
            y_begin = y
    dual, sums = call(
        z,
        part(last_kernel, z),
        (weight, *slots, *shared, y, y_begin),
        [line(z.rs), line(8)],
        [line(z.nr * z.rows)],
    )
    (final,) = call(
        z,
        part(weight_kernel, z),
        (weight, sums, *period_exchange(sums, True)),
        [(1,)],
        scalar=True,
    )
    return (x, dual, final.reshape(()))


def solution(mesh):
    in_specs = (
        P(("period", "row"), "col"),
        P(("period", "col"), "row"),
        P(("period", "row"), "col"),
        P(("period", "col"), "row"),
        P(("period", "row"), "col"),
        P(("period", "row"), "col"),
        P(("period", "col"), "row"),
        P("period", "row", "col", None, None, None),
        P("period", "row", "col", None),
        P("period", "row", "col", None),
        P("period", "row", "col", None, None),
    )
    out_specs = (P(("period", "row"), "col"), P(("period", "col"), "row"), P())
    return jax.shard_map(
        per_device, mesh=mesh, in_specs=in_specs, out_specs=out_specs, check_vma=False
    )
```

```python
import functools
import jax
import jax.numpy as jnp
from jax import lax
from jax.experimental import pallas as pl
from jax.experimental.pallas import tpu as pltpu
from jax.sharding import PartitionSpec as P

ROUNDS = 2
INNER = 2
STEP_SCALE = 0.15
EPSILON = 1e-06
F32 = jnp.float32
BF16 = jnp.bfloat16
FETCH = 49 << 20
AWAY = 59 << 20
FETCHES = 8


def up(n, m):
    return -(-n // m) * m


def peer(me, j, n):
    return me ^ j if n & (n - 1) == 0 else lax.rem(me + j, n)


def from_peer(x, axis, j):
    n = lax.axis_size(axis)
    pairs = [((i ^ j) if n & (n - 1) == 0 else (i + j) % n, i) for i in range(n)]
    return lax.ppermute(x, axis, pairs)


def exchange(x, axis):
    return [x] + [from_peer(x, axis, j) for j in range(1, lax.axis_size(axis))]


def period_exchange(x, all_of_them):
    n = lax.axis_size("period")
    if n % 2 == 0 and n > 2:
        even = {i: i ^ 1 for i in range(n)}
        odd = {i: ((i - 1) if i % 2 == 0 else (i + 1)) % n for i in range(n)}
        got = [lax.ppermute(x, "period", [(m[i], i) for i in range(n)]) for m in (even, odd)]
    else:
        got = [lax.ppermute(x, "period", [((i + s) % n, i) for i in range(n)]) for s in (1, n - 1)]
    if all_of_them:
        got += [
            lax.ppermute(x, "period", [((i + s) % n, i) for i in range(n)]) for s in range(2, n - 1)
        ]
    return got


def next_and_previous(first, second, size, me):
    if size % 2 == 0 and size > 2:
        is_even = lax.rem(me, 2) == 0
        return jnp.where(is_even, first, second), jnp.where(is_even, second, first)
    return first, second


def onehot(lists, first, count, height):
    spots = lax.broadcasted_iota(jnp.int32, (height, count), 0).astype(F32)
    return jnp.where(spots == lists[:, first : first + count], 1.0, 0.0).astype(BF16)


def total(x):
    return jnp.sum(jnp.sum(x, axis=0, keepdims=True), axis=1, keepdims=True)


class Sizes:
    def __init__(self, mesh_period, mesh_row, mesh_col, tile, listed, col_share, row_share):
        self.np, self.nr, self.nc = mesh_period, mesh_row, mesh_col
        self.tile, self.nt = tile, listed
        self.cs, self.rs = col_share, row_share
        self.cols, self.rows = col_share * mesh_row, row_share * mesh_col
        self.listed = self.nr * self.nt
        self.products = self.listed + self.nr
        self.blocks = -(-self.products // tile)
        self.zrows = up(self.products + 1, 8)
        self.ghosts = up(self.nr, 8)
        self.xrows = self.cols + self.ghosts
        self.hop = up(2 * self.nr + 2, 8)
        self.hop_first = self.hop + up(4 * self.nr, 8)
        self.group = tile // self.nt
        self.row_lists = -(-self.nc // self.group)
        self.setup = 3 * self.rows + up(self.row_lists + 2, 8)
        self.link = 4 * col_share + 8
        self.limit = (self.nr * listed * tile * tile * 4 * 3) // 2 + (10 << 20)


def copies(pairs, sems):
    started = [pltpu.make_async_copy(src, dst, sems.at[i]) for i, (src, dst) in enumerate(pairs)]
    for copy in started:
        copy.start()
    for copy in started:
        copy.wait()


def dual_message_kernel(z, dual_at, rhs_at, rkind_at, obj_at, rlist_at, zmsg, rkind, obj, rlist, sems):
    rs = z.rs
    copies(
        [
            (dual_at, zmsg.at[0:rs, :]),
            (rhs_at, zmsg.at[rs : 2 * rs, :]),
            (rkind_at, rkind),
            (obj_at, obj),
            (rlist_at, rlist),
        ],
        sems,
    )
    rhs = zmsg[rs : 2 * rs, :]
    zmsg[2 * rs : 3 * rs, :] = jnp.where(rkind[...] == 0, 0.0, -jnp.inf)
    zmsg[3 * rs : 3 * rs + 8, :] = jnp.zeros((8, z.tile), F32)
    zmsg[3 * rs : 3 * rs + 1, 0 : z.nt] = rlist[...].astype(F32)
    ones = jnp.ones((1, z.tile), F32)
    zmsg[3 * rs + 1 : 3 * rs + 2, :] = total(obj[...] * obj[...]) * ones
    zmsg[3 * rs + 2 : 3 * rs + 3, :] = total(rhs * rhs) * ones


def primal_message_kernel(
    z, x_at, obj_at, ub_at, ckind_at, clist_at, link_at, xmsg, ub, ckind, clist, sems
):
    cs = z.cs
    copies(
        [
            (x_at, xmsg.at[0:cs, :]),
            (obj_at, xmsg.at[cs : 2 * cs, :]),
            (ub_at, ub),
            (ckind_at, ckind),
            (clist_at, clist),
            (link_at, xmsg.at[z.link : z.link + z.tile, :]),
        ],
        sems,
    )
    kind = ckind[...]
    xmsg[2 * cs : 3 * cs, :] = jnp.where(kind == 2, -jnp.inf, 0.0)
    xmsg[3 * cs : 4 * cs, :] = jnp.where(kind == 1, ub[...], jnp.inf)
    xmsg[4 * cs : 4 * cs + 8, :] = jnp.zeros((8, z.tile), F32)
    xmsg[4 * cs : 4 * cs + 1, 0 : z.nt] = clist[...].astype(F32)


def two_parts(values):
    head = values.astype(BF16)
    return head, (values - head.astype(F32)).astype(BF16)


def fetch_kernel(z, tiles_at, tiles, heads, rests, token, sems):
    step = max(z.nt // FETCHES, 1)
    cuts = range(0, z.nt, step)
    started = [
        pltpu.make_async_copy(tiles_at.at[i : i + step], tiles.at[i : i + step], sems.at[c])
        for c, i in enumerate(cuts)
    ]
    for copy in started:
        copy.start()
    token[...] = jnp.zeros_like(token)
    for i, copy in zip(cuts, started):
        copy.wait()
        for n in range(i, i + step):
            heads[n], rests[n] = two_parts(tiles[n])


def turn_kernel(z, when, tiles, heads, rests):
    for n in range(z.nt):
        heads[n], rests[n] = two_parts(tiles[n].T)


def part_rows(values, pairs):
    head, rest = two_parts(values)
    count = values.shape[0]
    pairs[pl.ds(0, count, stride=2), :] = head.astype(F32)
    pairs[pl.ds(1, count, stride=2), :] = rest.astype(F32)


def row_times_tile(pairs, n, heads, rests):
    row = pairs[2 * n : 2 * n + 2, :].astype(BF16)
    main = jnp.dot(row, heads[n], preferred_element_type=F32)
    small = jnp.dot(row, rests[n], preferred_element_type=F32)
    return main[0:1] + (main[1:2] + small[0:1])


def put_list(z, lists, rows, i):
    lane = lax.broadcasted_iota(jnp.int32, (8, z.tile), 1)
    moved = pltpu.roll(rows, i * z.nt, 1) if i else rows
    return jnp.where(lane // z.nt == i, moved, lists)


def assemble_kernel(z, *refs):
    slots, out = refs[1:-1], refs[-1]
    me = lax.axis_index("col")
    base = 3 * z.rows
    out[base:, :] = jnp.zeros((z.setup - base, z.tile), F32)
    sums = jnp.zeros((2, z.tile), F32)
    lists = [jnp.zeros((8, z.tile), F32) for _ in range(z.row_lists)]
    for d, slot in enumerate(slots):
        at = peer(me, d, z.nc) * z.rs
        for part in range(3):
            spot = pl.ds(pl.multiple_of(part * z.rows + at, z.rs), z.rs)
            out[spot, :] = slot[part * z.rs : (part + 1) * z.rs, :]
        q = d // z.group
        lists[q] = put_list(z, lists[q], slot[3 * z.rs : 3 * z.rs + 8, :], d % z.group)
        sums = sums + slot[3 * z.rs + 1 : 3 * z.rs + 3, :]
    for q in range(z.row_lists):
        out[base + q : base + q + 1, :] = lists[q][0:1, :]
    out[base + z.row_lists : base + z.row_lists + 2, :] = sums


def three_parts(values):
    head = values.astype(BF16)
    rest = values - head.astype(F32)
    middle = rest.astype(BF16)
    return head, middle, (rest - middle.astype(F32)).astype(BF16)


def exact_dot(chosen, values):
    head, middle, tail = three_parts(values)
    dot = functools.partial(jnp.dot, preferred_element_type=F32)
    return dot(chosen, head) + (dot(chosen, middle) + dot(chosen, tail))


def exact_turned_dot(left, right):
    dot = lambda a, b: lax.dot_general(
        a, b, (((0,), (0,)), ((), ())), preferred_element_type=F32
    )
    if left.dtype == BF16:
        head, middle, tail = three_parts(right)
        return dot(left, head) + (dot(left, middle) + dot(left, tail))
    head, middle, tail = three_parts(left)
    return dot(head, right) + (dot(middle, right) + dot(tail, right))


def transposed_products(z, y_at, shared, tiles, parts, links, products, pairs):
    me = lax.axis_index("col")
    columns = []
    for j in range(z.nr):
        chosen = onehot(shared[j][3 * z.rows : 3 * z.rows + 1, :], 0, z.nt, z.rows)
        block = y_at[j * z.rows : (j + 1) * z.rows, :]
        if j == 0:
            part_rows(exact_turned_dot(chosen, block), pairs)
            columns.append(None)
        else:
            columns.append(exact_turned_dot(block, chosen))
    for n in range(z.nt):
        products[n : n + 1, :] = row_times_tile(pairs, n, *parts)
        for j in range(1, z.nr):
            k = j * z.nt + n
            column = columns[j][:, n : n + 1]
            products[k : k + 1, :] = jnp.sum(tiles[j][n] * column, axis=0, keepdims=True)
    for j in range(z.nr):
        first = y_at[pl.ds(j * z.rows + me * z.rs, 1), :]
        coupled = jnp.broadcast_to(first, (8, z.tile)).T
        k = z.listed + j
        link = links[j][z.link : z.link + z.tile, :]
        products[k : k + 1, :] = jnp.sum(link * coupled[:, 0:1], axis=0, keepdims=True)


def column_lists(z, halves, q):
    lists = jnp.zeros((8, z.tile), F32)
    for i in range(min(z.group, z.nr - q * z.group)):
        at = 4 * z.cs
        lists = put_list(z, lists, halves[q * z.group + i][at : at + 8, :], i)
    return lists[0:1, :]


def gradient_part(z, products, halves, g, msg, sums):
    row = lax.axis_index("row")
    full = jnp.zeros((z.cols, z.tile), F32)
    for q in range(-(-z.listed // z.tile)):
        count = min(z.tile, z.listed - q * z.tile)
        chosen = onehot(column_lists(z, halves, q), 0, count, z.cols)
        full = full + exact_dot(chosen, products[q * z.tile : q * z.tile + count, :])
    g[0 : z.cols, :] = full
    g[z.cols :, :] = jnp.zeros((z.ghosts, z.tile), F32)
    msg[...] = jnp.zeros_like(msg)
    for j in range(z.nr):
        outflow = products[z.listed + j : z.listed + j + 1, :]
        g[z.cols + j : z.cols + j + 1, :] = outflow
        msg[j : j + 1, :] = outflow
        last = peer(row, j, z.nr) * z.cs + z.cs - 1
        msg[z.nr + j : z.nr + j + 1, :] = g[pl.ds(last, 1), :]
    for i, value in enumerate(sums):
        msg[2 * z.nr + i : 2 * z.nr + i + 1, :] = value


def first_kernel(z, *refs):
    shared, refs = refs[: z.nr], refs[z.nr :]
    halves, refs = refs[: z.nr], refs[z.nr :]
    tiles, refs = (None, *refs[: z.nr - 1]), refs[z.nr - 1 :]
    parts, refs = refs[:2], refs[2:]
    y, xs, g, msg, products, pairs = refs
    row = lax.axis_index("row")
    for j in range(z.nr):
        y[j * z.rows : (j + 1) * z.rows, :] = shared[j][0 : z.rows, :]
        at = peer(row, j, z.nr) * z.cs
        for part in range(4):
            spot = pl.ds(pl.multiple_of(part * z.xrows + at, 8), z.cs)
            xs[spot, :] = halves[j][part * z.cs : (part + 1) * z.cs, :]
    transposed_products(z, y, shared, tiles, parts, halves, products, pairs)
    base = 3 * z.rows + z.row_lists
    sums = [sum(s[base + i : base + i + 1, :] for s in shared) for i in range(2)]
    gradient_part(z, products, halves, g, msg, sums)
    for part in range(4):
        xs[part * z.xrows + z.cols : (part + 1) * z.xrows, :] = jnp.zeros((z.ghosts, z.tile), F32)
        for j in range(z.nr):
            to = z.hop + part * z.nr + j
            msg[to : to + 1, :] = halves[j][(part + 1) * z.cs - 1 : (part + 1) * z.cs, :]


def dual_part(z, w, slots, shared, y_old, y_out):
    me = lax.axis_index("col")
    sigma = STEP_SCALE * w[0:1, :]
    for j in range(z.nr):
        summed = jnp.zeros((z.rows, z.tile), F32)
        for q in range(z.row_lists):
            ds = range(q * z.group, min((q + 1) * z.group, z.nc))
            lists = shared[j][3 * z.rows + q : 3 * z.rows + q + 1, :]
            chosen = onehot(lists, 0, len(ds) * z.nt, z.rows)
            parts = [slots[d][j * z.nt : (j + 1) * z.nt, :] for d in ds]
            summed = summed + exact_dot(chosen, jnp.concatenate(parts, axis=0))
        spot = slice(j * z.rows, (j + 1) * z.rows)
        y_out[spot, :] = summed
        for d in range(z.nc):
            at = pl.ds(j * z.rows + peer(me, d, z.nc) * z.rs, 1)
            y_out[at, :] = y_out[at, :] + slots[d][z.listed + j : z.listed + j + 1, :]
        moved = y_old[spot, :] + sigma * (shared[j][z.rows : 2 * z.rows, :] - y_out[spot, :])
        y_out[spot, :] = jnp.maximum(moved, shared[j][2 * z.rows : 3 * z.rows, :])


def mean_and_move(now, before, begin):
    mean = (now + before) * (1.0 / INNER)
    return mean, total((mean - begin) * (mean - begin))


def dual_kernel(z, ends, *refs):
    w, refs = refs[0], refs[1:]
    slots, refs = refs[: z.nc], refs[z.nc :]
    shared, refs = refs[: z.nr], refs[z.nr :]
    halves, refs = refs[: z.nr], refs[z.nr :]
    tiles, refs = (None, *refs[: z.nr - 1]), refs[z.nr - 1 :]
    parts, refs = refs[:2], refs[2:]
    y_old = refs[0]
    y_begin = refs[1] if ends else None
    y_out, g, msg, products, pairs = refs[-5:]
    dual_part(z, w, slots, shared, y_old, y_out)
    sums = []
    if ends:
        mean, move = mean_and_move(y_out[...], y_old[...], y_begin[...])
        y_out[...] = mean
        moved = sum(s[z.products : z.products + 1, :] for s in slots)
        sums = [moved, move * jnp.ones((1, z.tile), F32)]
    transposed_products(z, y_out, shared, tiles, parts, halves, products, pairs)
    gradient_part(z, products, halves, g, msg, sums)


def last_kernel(z, *refs):
    w, refs = refs[0], refs[1:]
    slots, refs = refs[: z.nc], refs[z.nc :]
    shared, refs = refs[: z.nr], refs[z.nr :]
    y_old, y_begin, out, msg, y_new = refs
    dual_part(z, w, slots, shared, y_old, y_new)
    mean, move = mean_and_move(y_new[...], y_old[...], y_begin[...])
    y_new[...] = mean
    me = lax.axis_index("col")
    out[...] = y_new[pl.ds(pl.multiple_of(me * z.rs, z.rs), z.rs), :]
    msg[...] = jnp.zeros_like(msg)
    msg[0:1, :] = sum(s[z.products : z.products + 1, :] for s in slots)
    msg[1:2, :] = move * jnp.ones((1, z.tile), F32)


def weight_kernel(z, *refs):
    w, msgs, out = refs[0], refs[1:-1], refs[-1]
    dx = sum(m[0:1, :] for m in msgs)
    dy = sum(m[1:2, :] for m in msgs)
    new = jnp.sqrt(w[0:1, :] * jnp.sqrt((dx + EPSILON) / (dy + EPSILON)))
    out[0] = new[0, 0]


def primal_kernel(z, starts, first, ends, last, *refs):
    w_old, refs = (None, refs) if first else (refs[0], refs[1:])
    g, own, refs = refs[0], refs[1], refs[2:]
    count = (z.np - 1) if starts else 2
    got, refs = refs[:count], refs[count:]
    xs, refs = refs[0], refs[1:]
    x_old, refs = (None, refs) if first else (refs[0], refs[1:])
    x_begin, refs = (refs[0], refs[1:]) if ends else (None, refs)
    halves, refs = refs[: z.nr], refs[z.nr :]
    tiles, refs = (None, *refs[: z.nr - 1]), refs[z.nr - 1 :]
    parts, refs = refs[:2], refs[2:]
    x_out, zmsg, refs = refs[0], refs[1], refs[2:]
    w_out, refs = (refs[0], refs[1:]) if starts else (None, refs)
    xs_out, refs = (refs[0], refs[1:]) if first else (None, refs)
    work, v, vectors, pairs = refs
    period, row = lax.axis_index("period"), lax.axis_index("row")

    if starts:
        s1 = own[2 * z.nr : 2 * z.nr + 1, :]
        s2 = own[2 * z.nr + 1 : 2 * z.nr + 2, :]
        for m in got:
            s1 = s1 + m[2 * z.nr : 2 * z.nr + 1, :]
            s2 = s2 + m[2 * z.nr + 1 : 2 * z.nr + 2, :]
        ratio = (s1 + EPSILON) / (s2 + EPSILON)
        weight = jnp.sqrt(ratio) if first else jnp.sqrt(w_old[0:1, :] * jnp.sqrt(ratio))
        w_out[...] = jnp.broadcast_to(weight, w_out.shape)
    else:
        weight = w_old[0:1, :]
    tau = STEP_SCALE / weight

    after, before = next_and_previous(got[0][...], got[1][...], z.np, period)
    has_next = period < z.np - 1
    has_previous = period > 0
    work[...] = g[...]
    for j in range(z.nr):
        last_row = pl.ds(peer(row, j, z.nr) * z.cs + z.cs - 1, 1)
        outflow = jnp.where(has_next, after[j : j + 1, :], 0.0)
        work[last_row, :] = work[last_row, :] + outflow
        ghost = slice(z.cols + j, z.cols + j + 1)
        work[ghost, :] = work[ghost, :] + before[z.nr + j : z.nr + j + 1, :]
    if first:
        xs_out[...] = xs[...]
        for part in range(4):
            for j in range(z.nr):
                to = part * z.xrows + z.cols + j
                at = z.hop + part * z.nr + j
                xs_out[to : to + 1, :] = before[at : at + 1, :]
        data = xs_out
        x_now = xs_out[0 : z.xrows, :]
    else:
        data = xs
        x_now = x_old[...]
    obj = data[z.xrows : 2 * z.xrows, :]
    low = data[2 * z.xrows : 3 * z.xrows, :]
    high = data[3 * z.xrows : 4 * z.xrows, :]
    x_new = jnp.minimum(jnp.maximum(x_now - tau * (obj - work[...]), low), high)
    v[...] = 2.0 * x_new - x_now
    v[z.cols :, :] = jnp.where(has_previous, v[z.cols :, :], 0.0)
    move = None
    if ends:
        mean = (x_new + x_now) * (1.0 / INNER)
        moved = mean[0 : z.cols, :] - x_begin[0 : z.cols, :]
        move = total(moved * moved)
        if last:
            work[...] = mean
            x_out[...] = work[pl.ds(pl.multiple_of(row * z.cs, z.cs), z.cs), :]
        else:
            x_out[...] = mean
    else:
        x_out[...] = x_new

    for q in range(-(-z.listed // z.tile)):
        count = min(z.tile, z.listed - q * z.tile)
        chosen = onehot(column_lists(z, halves, q), 0, count, z.cols)
        vectors[q * z.tile : q * z.tile + count, :] = exact_turned_dot(chosen, v[0 : z.cols, :])
    part_rows(vectors[0 : z.nt, :], pairs)
    lane = lax.broadcasted_iota(jnp.int32, (z.tile, z.tile), 1)
    rows = []
    for b in range(z.blocks):
        columns = jnp.zeros((z.tile, z.tile), F32)
        for k in range(b * z.tile, min((b + 1) * z.tile, z.products)):
            if k < z.nt:
                continue
            if k < 2 * z.nt:
                rows.append(row_times_tile(pairs, k - z.nt, *parts))
            if k < z.listed:
                tile = tiles[k // z.nt][k % z.nt]
                vector = vectors[k : k + 1, :]
            else:
                tile = halves[k - z.listed][z.link : z.link + z.tile, :]
                vector = v[z.cols + k - z.listed : z.cols + k - z.listed + 1, :]
            column = jnp.sum(tile * vector, axis=1, keepdims=True)
            columns = jnp.where(lane == k % z.tile, column, columns)
        count = min(z.zrows - b * z.tile, z.tile)
        zmsg[b * z.tile : b * z.tile + count, :] = columns.T[0:count, :]
    for n, row_n in enumerate(rows):
        zmsg[n : n + 1, :] = row_n
    if ends:
        zmsg[z.products : z.products + 1, :] = move * jnp.ones((1, z.tile), F32)


def typed(shapes):
    return [s if isinstance(s[0], tuple) else (s, F32) for s in shapes]


def call(z, kernel, operands, shapes, scratch=(), away=0, sems=0, scalar=False, limit=None):
    spaces = [pl.ANY] * away + [pltpu.VMEM] * (len(operands) - away)
    return pl.pallas_call(
        kernel,
        out_shape=[jax.ShapeDtypeStruct(s, kind) for s, kind in typed(shapes)],
        in_specs=[pl.BlockSpec(memory_space=s) for s in spaces],
        out_specs=[
            pl.BlockSpec(memory_space=pltpu.SMEM if scalar else pltpu.VMEM) for _ in shapes
        ],
        scratch_shapes=[pltpu.VMEM(s, kind) for s, kind in typed(scratch)]
        + ([pltpu.SemaphoreType.DMA((sems,))] if sems else []),
        compiler_params=pltpu.CompilerParams(vmem_limit_bytes=limit or z.limit),
    )(*operands)


def per_device(
    primal_start,
    dual_start,
    objective,
    right_side,
    upper_bound,
    column_kind,
    row_kind,
    tile_values,
    tile_rows,
    tile_cols,
    coupling,
):
    tile = tile_values.shape[-1]
    listed = tile_values.shape[3]
    z = Sizes(
        lax.axis_size("period"),
        lax.axis_size("row"),
        lax.axis_size("col"),
        tile,
        listed,
        primal_start.shape[0],
        dual_start.shape[0],
    )
    part = functools.partial
    line = lambda rows: (rows, tile)
    row_list = tile_rows.reshape(1, listed)
    col_list = tile_cols.reshape(1, listed)
    tiles_away = tile_values.reshape(listed, tile, tile)
    tiles = exchange(tiles_away, "row")
    (zmsg,) = call(
        z,
        part(dual_message_kernel, z),
        (dual_start, right_side, row_kind, objective, row_list),
        [line(3 * z.rs + 8)],
        [(line(z.rs), jnp.int32), line(z.cs), ((1, listed), jnp.int32)],
        away=5,
        sems=5,
        limit=AWAY,
    )
    (xmsg,) = call(
        z,
        part(primal_message_kernel, z),
        (
            primal_start,
            objective,
            upper_bound,
            column_kind,
            col_list,
            coupling.reshape(tile, tile),
        ),
        [line(z.link + tile)],
        [line(z.cs), (line(z.cs), jnp.int32), ((1, listed), jnp.int32)],
        away=6,
        sems=6,
        limit=AWAY,
    )
    block = (listed, tile, tile)
    own_tiles, heads, rests, token = call(
        z,
        part(fetch_kernel, z),
        (tiles_away,),
        [block, (block, BF16), (block, BF16), line(8)],
        away=1,
        sems=FETCHES,
        limit=FETCH,
    )
    slots = exchange(zmsg, "col")
    halves = exchange(xmsg, "row")
    (gathered,) = call(z, part(assemble_kernel, z), [token] + slots, [line(z.setup)])
    shared = exchange(gathered, "row")

    products = line(up(z.products, 8))
    y, xs, g, msg = call(
        z,
        part(first_kernel, z),
        (*shared, *halves, *tiles[1:], heads, rests),
        [line(z.nr * z.rows), line(4 * z.xrows), line(z.xrows), line(z.hop_first)],
        [products, line(2 * listed)],
    )
    turned = call(z, part(turn_kernel, z), (g, own_tiles), [(block, BF16), (block, BF16)])
    x = None
    weight = None
    y_begin, x_begin = y, None
    for step in range(ROUNDS * INNER):
        starts = step % INNER == 0
        ends = step % INNER == INNER - 1
        first, last = step == 0, step == ROUNDS * INNER - 1
        got = period_exchange(msg, starts)
        operands = ([] if first else [weight]) + [g, msg, *got, xs]
        operands += ([] if first else [x]) + ([x_begin] if ends else []) + [*halves, *tiles[1:], *turned]
        shapes = [line(z.cs if last else z.xrows), line(z.zrows)]
        shapes += ([line(8)] if starts else []) + ([line(4 * z.xrows)] if first else [])
        outs = call(
            z,
            part(primal_kernel, z, starts, first, ends, last),
            operands,
            shapes,
            [line(z.xrows), line(z.xrows), line(up(z.listed, 8)), line(2 * listed)],
        )
        x_next, zmsg = outs[:2]
        if starts:
            weight = outs[2]
        if first:
            xs = outs[3]
            x = xs[0 : z.xrows]
        if starts:
            x_begin = x
        x = x_next
        slots = exchange(zmsg, "col")
        if last:
            break
        operands = [weight, *slots, *shared, *halves, *tiles[1:], heads, rests, y]
        y_next, g, msg = call(
            z,
            part(dual_kernel, z, ends),
            operands + ([y_begin] if ends else []),
            [line(z.nr * z.rows), line(z.xrows), line(z.hop)],
            [products, line(2 * listed)],
        )
        y = y_next
        if ends:
            y_begin = y
    dual, sums = call(
        z,
        part(last_kernel, z),
        (weight, *slots, *shared, y, y_begin),
        [line(z.rs), line(8)],
        [line(z.nr * z.rows)],
    )
    (final,) = call(
        z,
        part(weight_kernel, z),
        (weight, sums, *period_exchange(sums, True)),
        [(1,)],
        scalar=True,
    )
    return (x, dual, final.reshape(()))


def solution(mesh):
    in_specs = (
        P(("period", "row"), "col"),
        P(("period", "col"), "row"),
        P(("period", "row"), "col"),
        P(("period", "col"), "row"),
        P(("period", "row"), "col"),
        P(("period", "row"), "col"),
        P(("period", "col"), "row"),
        P("period", "row", "col", None, None, None),
        P("period", "row", "col", None),
        P("period", "row", "col", None),
        P("period", "row", "col", None, None),
    )
    out_specs = (P(("period", "row"), "col"), P(("period", "col"), "row"), P())
    return jax.shard_map(
        per_device, mesh=mesh, in_specs=in_specs, out_specs=out_specs, check_vma=False
    )
```

```python
import functools
import jax
import jax.numpy as jnp
from jax import lax
from jax.experimental import pallas as pl
from jax.experimental.pallas import tpu as pltpu
from jax.sharding import PartitionSpec as P

ROUNDS = 2
INNER = 2
STEP_SCALE = 0.15
EPSILON = 1e-06
F32 = jnp.float32
BF16 = jnp.bfloat16
FETCH = 49 << 20
AWAY = 59 << 20
FETCHES = 8


def up(n, m):
    return -(-n // m) * m


def peer(me, j, n):
    return me ^ j if n & (n - 1) == 0 else lax.rem(me + j, n)


def from_peer(x, axis, j):
    n = lax.axis_size(axis)
    pairs = [((i ^ j) if n & (n - 1) == 0 else (i + j) % n, i) for i in range(n)]
    return lax.ppermute(x, axis, pairs)


def exchange(x, axis):
    return [x] + [from_peer(x, axis, j) for j in range(1, lax.axis_size(axis))]


def period_exchange(x, all_of_them):
    n = lax.axis_size("period")
    if n % 2 == 0 and n > 2:
        even = {i: i ^ 1 for i in range(n)}
        odd = {i: ((i - 1) if i % 2 == 0 else (i + 1)) % n for i in range(n)}
        got = [lax.ppermute(x, "period", [(m[i], i) for i in range(n)]) for m in (even, odd)]
    else:
        got = [lax.ppermute(x, "period", [((i + s) % n, i) for i in range(n)]) for s in (1, n - 1)]
    if all_of_them:
        got += [
            lax.ppermute(x, "period", [((i + s) % n, i) for i in range(n)]) for s in range(2, n - 1)
        ]
    return got


def next_and_previous(first, second, size, me):
    if size % 2 == 0 and size > 2:
        is_even = lax.rem(me, 2) == 0
        return jnp.where(is_even, first, second), jnp.where(is_even, second, first)
    return first, second


def onehot(lists, first, count, height):
    spots = lax.broadcasted_iota(jnp.int32, (height, count), 0).astype(F32)
    return jnp.where(spots == lists[:, first : first + count], 1.0, 0.0).astype(BF16)


def total(x):
    return jnp.sum(jnp.sum(x, axis=0, keepdims=True), axis=1, keepdims=True)


class Sizes:
    def __init__(self, mesh_period, mesh_row, mesh_col, tile, listed, col_share, row_share):
        self.np, self.nr, self.nc = mesh_period, mesh_row, mesh_col
        self.tile, self.nt = tile, listed
        self.cs, self.rs = col_share, row_share
        self.cols, self.rows = col_share * mesh_row, row_share * mesh_col
        self.listed = self.nr * self.nt
        self.products = self.listed + self.nr
        self.blocks = -(-self.products // tile)
        self.zrows = up(self.products + 1, 8)
        self.ghosts = up(self.nr, 8)
        self.xrows = self.cols + self.ghosts
        self.hop = up(2 * self.nr + 2, 8)
        self.hop_first = self.hop + up(4 * self.nr, 8)
        self.group = tile // self.nt
        self.row_lists = -(-self.nc // self.group)
        self.setup = 3 * self.rows + up(self.row_lists + 2, 8)
        self.link = 4 * col_share + 8
        self.limit = (self.nr * listed * tile * tile * 4 * 3) // 2 + (10 << 20)


def copies(pairs, sems):
    started = [pltpu.make_async_copy(src, dst, sems.at[i]) for i, (src, dst) in enumerate(pairs)]
    for copy in started:
        copy.start()
    for copy in started:
        copy.wait()


def dual_message_kernel(z, dual_at, rhs_at, rkind_at, obj_at, rlist_at, zmsg, rkind, obj, rlist, sems):
    rs = z.rs
    copies(
        [
            (dual_at, zmsg.at[0:rs, :]),
            (rhs_at, zmsg.at[rs : 2 * rs, :]),
            (rkind_at, rkind),
            (obj_at, obj),
            (rlist_at, rlist),
        ],
        sems,
    )
    rhs = zmsg[rs : 2 * rs, :]
    zmsg[2 * rs : 3 * rs, :] = jnp.where(rkind[...] == 0, 0.0, -jnp.inf)
    zmsg[3 * rs : 3 * rs + 8, :] = jnp.zeros((8, z.tile), F32)
    zmsg[3 * rs : 3 * rs + 1, 0 : z.nt] = rlist[...].astype(F32)
    ones = jnp.ones((1, z.tile), F32)
    zmsg[3 * rs + 1 : 3 * rs + 2, :] = total(obj[...] * obj[...]) * ones
    zmsg[3 * rs + 2 : 3 * rs + 3, :] = total(rhs * rhs) * ones


def primal_message_kernel(
    z, x_at, obj_at, ub_at, ckind_at, clist_at, link_at, xmsg, ub, ckind, clist, sems
):
    cs = z.cs
    copies(
        [
            (x_at, xmsg.at[0:cs, :]),
            (obj_at, xmsg.at[cs : 2 * cs, :]),
            (ub_at, ub),
            (ckind_at, ckind),
            (clist_at, clist),
            (link_at, xmsg.at[z.link : z.link + z.tile, :]),
        ],
        sems,
    )
    kind = ckind[...]
    xmsg[2 * cs : 3 * cs, :] = jnp.where(kind == 2, -jnp.inf, 0.0)
    xmsg[3 * cs : 4 * cs, :] = jnp.where(kind == 1, ub[...], jnp.inf)
    xmsg[4 * cs : 4 * cs + 8, :] = jnp.zeros((8, z.tile), F32)
    xmsg[4 * cs : 4 * cs + 1, 0 : z.nt] = clist[...].astype(F32)


def two_parts(values):
    head = values.astype(BF16)
    return head, (values - head.astype(F32)).astype(BF16)


def put_parts(wide, values):
    tile = values.shape[-1]
    wide[:, 0:tile], wide[:, tile : 2 * tile] = two_parts(values)


def fetch_kernel(z, tiles_at, tiles, wide, token, sems):
    step = max(z.nt // FETCHES, 1)
    cuts = range(0, z.nt, step)
    started = [
        pltpu.make_async_copy(tiles_at.at[i : i + step], tiles.at[i : i + step], sems.at[c])
        for c, i in enumerate(cuts)
    ]
    for copy in started:
        copy.start()
    token[...] = jnp.zeros_like(token)
    for i, copy in zip(cuts, started):
        copy.wait()
        for n in range(i, i + step):
            put_parts(wide.at[n], tiles[n])


def turn_kernel(z, when, tiles, sibling, turned, sibling_wide, sibling_turned):
    for n in range(z.nt):
        put_parts(turned.at[n], tiles[n].T)
    for n in range(z.nt // 2):
        put_parts(sibling_wide.at[n], sibling[n])
        put_parts(sibling_turned.at[n], sibling[n].T)


def part_rows(values, pairs, first):
    head, rest = two_parts(values)
    count = values.shape[0]
    pairs[pl.ds(2 * first, count, stride=2), :] = head.astype(F32)
    pairs[pl.ds(2 * first + 1, count, stride=2), :] = rest.astype(F32)


def row_times_tile(z, pairs, k, wide):
    row = pairs[2 * k : 2 * k + 2, :].astype(BF16)
    product = jnp.dot(row, wide[k // z.nt][k % z.nt], preferred_element_type=F32)
    head, rest = product[:, 0 : z.tile], product[:, z.tile : 2 * z.tile]
    return head[0:1] + (head[1:2] + rest[0:1])


def two_units(matrix, vector):
    jobs = [((i + 0.5) / len(matrix), 0, k) for i, k in enumerate(matrix)]
    jobs += [((i + 0.5) / len(vector), 1, k) for i, k in enumerate(vector)]
    return [(kind == 0, k) for _, kind, k in sorted(jobs)]


def put_list(z, lists, rows, i):
    lane = lax.broadcasted_iota(jnp.int32, (8, z.tile), 1)
    moved = pltpu.roll(rows, i * z.nt, 1) if i else rows
    return jnp.where(lane // z.nt == i, moved, lists)


def assemble_kernel(z, *refs):
    slots, out = refs[-2:0:-1], refs[-1]
    me = lax.axis_index("col")
    base = 3 * z.rows
    out[base:, :] = jnp.zeros((z.setup - base, z.tile), F32)
    sums = jnp.zeros((2, z.tile), F32)
    lists = [jnp.zeros((8, z.tile), F32) for _ in range(z.row_lists)]
    for d, slot in enumerate(slots):
        at = peer(me, d, z.nc) * z.rs
        for part in range(3):
            spot = pl.ds(pl.multiple_of(part * z.rows + at, z.rs), z.rs)
            out[spot, :] = slot[part * z.rs : (part + 1) * z.rs, :]
        q = d // z.group
        lists[q] = put_list(z, lists[q], slot[3 * z.rs : 3 * z.rs + 8, :], d % z.group)
        sums = sums + slot[3 * z.rs + 1 : 3 * z.rs + 3, :]
    for q in range(z.row_lists):
        out[base + q : base + q + 1, :] = lists[q][0:1, :]
    out[base + z.row_lists : base + z.row_lists + 2, :] = sums


def three_parts(values):
    head = values.astype(BF16)
    rest = values - head.astype(F32)
    middle = rest.astype(BF16)
    return head, middle, (rest - middle.astype(F32)).astype(BF16)


def exact_dot(chosen, values):
    head, middle, tail = three_parts(values)
    dot = functools.partial(jnp.dot, preferred_element_type=F32)
    return dot(chosen, head) + (dot(chosen, middle) + dot(chosen, tail))


def exact_turned_dot(left, right):
    dot = lambda a, b: lax.dot_general(
        a, b, (((0,), (0,)), ((), ())), preferred_element_type=F32
    )
    if left.dtype == BF16:
        head, middle, tail = three_parts(right)
        return dot(left, head) + (dot(left, middle) + dot(left, tail))
    head, middle, tail = three_parts(left)
    return dot(head, right) + (dot(middle, right) + dot(tail, right))


def transposed_products(z, y_at, shared, tiles, wide, links, products, pairs):
    me = lax.axis_index("col")
    columns, on_matrix, on_vector = [], [], []
    for j in range(z.nr):
        lists = shared[j][3 * z.rows : 3 * z.rows + 1, :]
        block = y_at[j * z.rows : (j + 1) * z.rows, :]
        wides = wide[j].shape[0] if j < len(wide) else 0
        columns.append((None, wides))
        if wides:
            chosen = onehot(lists, 0, wides, z.rows)
            part_rows(exact_turned_dot(chosen, block), pairs, j * z.nt)
        if wides < z.nt:
            chosen = onehot(lists, wides, z.nt - wides, z.rows)
            columns[j] = (exact_turned_dot(block, chosen), wides)
        on_matrix += range(j * z.nt, j * z.nt + wides)
        on_vector += range(j * z.nt + wides, (j + 1) * z.nt)
    for matrix, k in two_units(on_matrix, on_vector):
        j, n = k // z.nt, k % z.nt
        if matrix:
            products[k : k + 1, :] = row_times_tile(z, pairs, k, wide)
        else:
            block, skip = columns[j]
            column = block[:, n - skip : n - skip + 1]
            products[k : k + 1, :] = jnp.sum(tiles[j][n] * column, axis=0, keepdims=True)
    for j in range(z.nr):
        first = y_at[pl.ds(j * z.rows + me * z.rs, 1), :]
        coupled = jnp.broadcast_to(first, (8, z.tile)).T
        k = z.listed + j
        link = links[j][z.link : z.link + z.tile, :]
        products[k : k + 1, :] = jnp.sum(link * coupled[:, 0:1], axis=0, keepdims=True)


def column_lists(z, halves, q):
    lists = jnp.zeros((8, z.tile), F32)
    for i in range(min(z.group, z.nr - q * z.group)):
        at = 4 * z.cs
        lists = put_list(z, lists, halves[q * z.group + i][at : at + 8, :], i)
    return lists[0:1, :]


def gradient_part(z, products, halves, g, msg, sums):
    row = lax.axis_index("row")
    full = jnp.zeros((z.cols, z.tile), F32)
    for q in range(-(-z.listed // z.tile)):
        count = min(z.tile, z.listed - q * z.tile)
        chosen = onehot(column_lists(z, halves, q), 0, count, z.cols)
        full = full + exact_dot(chosen, products[q * z.tile : q * z.tile + count, :])
    g[0 : z.cols, :] = full
    g[z.cols :, :] = jnp.zeros((z.ghosts, z.tile), F32)
    msg[...] = jnp.zeros_like(msg)
    for j in range(z.nr):
        outflow = products[z.listed + j : z.listed + j + 1, :]
        g[z.cols + j : z.cols + j + 1, :] = outflow
        msg[j : j + 1, :] = outflow
        last = peer(row, j, z.nr) * z.cs + z.cs - 1
        msg[z.nr + j : z.nr + j + 1, :] = g[pl.ds(last, 1), :]
    for i, value in enumerate(sums):
        msg[2 * z.nr + i : 2 * z.nr + i + 1, :] = value


def first_kernel(z, *refs):
    shared, refs = refs[: z.nr], refs[z.nr :]
    halves, refs = refs[: z.nr], refs[z.nr :]
    tiles, refs = (None, *refs[: z.nr - 1]), refs[z.nr - 1 :]
    wide, refs = refs[:1], refs[1:]
    y, xs, g, msg, products, pairs = refs
    row = lax.axis_index("row")
    for j in range(z.nr):
        y[j * z.rows : (j + 1) * z.rows, :] = shared[j][0 : z.rows, :]
        at = peer(row, j, z.nr) * z.cs
        for part in range(4):
            spot = pl.ds(pl.multiple_of(part * z.xrows + at, 8), z.cs)
            xs[spot, :] = halves[j][part * z.cs : (part + 1) * z.cs, :]
    transposed_products(z, y, shared, tiles, wide, halves, products, pairs)
    base = 3 * z.rows + z.row_lists
    sums = [sum(s[base + i : base + i + 1, :] for s in shared) for i in range(2)]
    gradient_part(z, products, halves, g, msg, sums)
    for part in range(4):
        xs[part * z.xrows + z.cols : (part + 1) * z.xrows, :] = jnp.zeros((z.ghosts, z.tile), F32)
        for j in range(z.nr):
            to = z.hop + part * z.nr + j
            msg[to : to + 1, :] = halves[j][(part + 1) * z.cs - 1 : (part + 1) * z.cs, :]


def dual_part(z, w, slots, shared, y_old, y_out):
    me = lax.axis_index("col")
    sigma = STEP_SCALE * w[0:1, :]
    spots = lax.broadcasted_iota(jnp.int32, (z.rows, z.tile), 0)
    for j in range(z.nr):
        summed = jnp.zeros((z.rows, z.tile), F32)
        for q in range(z.row_lists):
            ds = range(q * z.group, min((q + 1) * z.group, z.nc))
            lists = shared[j][3 * z.rows + q : 3 * z.rows + q + 1, :]
            chosen = onehot(lists, 0, len(ds) * z.nt, z.rows)
            parts = [slots[d][j * z.nt : (j + 1) * z.nt, :] for d in ds]
            summed = summed + exact_dot(chosen, jnp.concatenate(parts, axis=0))
        for d in range(z.nc):
            inflow = slots[d][z.listed + j : z.listed + j + 1, :]
            summed = summed + jnp.where(spots == peer(me, d, z.nc) * z.rs, inflow, 0.0)
        spot = slice(j * z.rows, (j + 1) * z.rows)
        moved = y_old[spot, :] + sigma * (shared[j][z.rows : 2 * z.rows, :] - summed)
        y_out[spot, :] = jnp.maximum(moved, shared[j][2 * z.rows : 3 * z.rows, :])


def mean_and_move(now, before, begin):
    mean = (now + before) * (1.0 / INNER)
    return mean, total((mean - begin) * (mean - begin))


def dual_kernel(z, ends, order, *refs):
    w, refs = refs[0], refs[1:]
    slots, refs = [refs[order.index(d)] for d in range(z.nc)], refs[z.nc :]
    shared, refs = refs[: z.nr], refs[z.nr :]
    halves, refs = refs[: z.nr], refs[z.nr :]
    tiles, refs = (None, *refs[: z.nr - 1]), refs[z.nr - 1 :]
    wide, refs = refs[:2], refs[2:]
    y_old = refs[0]
    y_begin = refs[1] if ends else None
    y_out, g, msg, products, pairs = refs[-5:]
    dual_part(z, w, slots, shared, y_old, y_out)
    sums = []
    if ends:
        mean, move = mean_and_move(y_out[...], y_old[...], y_begin[...])
        y_out[...] = mean
        moved = sum(s[z.products : z.products + 1, :] for s in slots)
        sums = [moved, move * jnp.ones((1, z.tile), F32)]
    transposed_products(z, y_out, shared, tiles, wide, halves, products, pairs)
    gradient_part(z, products, halves, g, msg, sums)


def last_kernel(z, *refs):
    w, refs = refs[0], refs[1:]
    slots, refs = refs[: z.nc][::-1], refs[z.nc :]
    shared, refs = refs[: z.nr], refs[z.nr :]
    y_old, y_begin, y_mean, msg, y_new = refs
    dual_part(z, w, slots, shared, y_old, y_new)
    mean, move = mean_and_move(y_new[...], y_old[...], y_begin[...])
    y_mean[...] = mean
    msg[...] = jnp.zeros_like(msg)
    msg[0:1, :] = sum(s[z.products : z.products + 1, :] for s in slots)
    msg[1:2, :] = move * jnp.ones((1, z.tile), F32)


def output_kernel(z, x, y, x_out, y_out, token):
    row, col = lax.axis_index("row"), lax.axis_index("col")
    x_out[...] = x[pl.ds(pl.multiple_of(row * z.cs, z.cs), z.cs), :]
    y_out[...] = y[pl.ds(pl.multiple_of(col * z.rs, z.rs), z.rs), :]
    token[...] = jnp.zeros_like(token)


def weight_kernel(z, *refs):
    w, msgs, out = refs[1], refs[2:-1], refs[-1]
    dx = sum(m[0:1, :] for m in msgs)
    dy = sum(m[1:2, :] for m in msgs)
    new = jnp.sqrt(w[0:1, :] * jnp.sqrt((dx + EPSILON) / (dy + EPSILON)))
    out[0] = new[0, 0]


def primal_kernel(z, starts, first, ends, *refs):
    w_old, refs = (None, refs) if first else (refs[0], refs[1:])
    g, own, refs = refs[0], refs[1], refs[2:]
    count = (z.np - 1) if starts else 2
    got, refs = refs[:count][::-1], refs[count:]
    xs, refs = refs[0], refs[1:]
    x_old, refs = (None, refs) if first else (refs[0], refs[1:])
    x_begin, refs = (refs[0], refs[1:]) if ends else (None, refs)
    halves, refs = refs[: z.nr], refs[z.nr :]
    tiles, refs = (None, *refs[: z.nr - 1]), refs[z.nr - 1 :]
    wide, refs = refs[:2], refs[2:]
    x_out, zmsg, refs = refs[0], refs[1], refs[2:]
    w_out, refs = (refs[0], refs[1:]) if starts else (None, refs)
    xs_out, refs = (refs[0], refs[1:]) if first else (None, refs)
    work, v, vectors, pairs = refs
    period, row = lax.axis_index("period"), lax.axis_index("row")

    if starts:
        s1 = own[2 * z.nr : 2 * z.nr + 1, :]
        s2 = own[2 * z.nr + 1 : 2 * z.nr + 2, :]
        for m in got:
            s1 = s1 + m[2 * z.nr : 2 * z.nr + 1, :]
            s2 = s2 + m[2 * z.nr + 1 : 2 * z.nr + 2, :]
        ratio = (s1 + EPSILON) / (s2 + EPSILON)
        weight = jnp.sqrt(ratio) if first else jnp.sqrt(w_old[0:1, :] * jnp.sqrt(ratio))
        w_out[...] = jnp.broadcast_to(weight, w_out.shape)
    else:
        weight = w_old[0:1, :]
    tau = STEP_SCALE / weight

    after, before = next_and_previous(got[0][...], got[1][...], z.np, period)
    has_next = period < z.np - 1
    has_previous = period > 0
    work[...] = g[...]
    for j in range(z.nr):
        last_row = pl.ds(peer(row, j, z.nr) * z.cs + z.cs - 1, 1)
        outflow = jnp.where(has_next, after[j : j + 1, :], 0.0)
        work[last_row, :] = work[last_row, :] + outflow
        ghost = slice(z.cols + j, z.cols + j + 1)
        work[ghost, :] = work[ghost, :] + before[z.nr + j : z.nr + j + 1, :]
    if first:
        xs_out[...] = xs[...]
        for part in range(4):
            for j in range(z.nr):
                to = part * z.xrows + z.cols + j
                at = z.hop + part * z.nr + j
                xs_out[to : to + 1, :] = before[at : at + 1, :]
        data = xs_out
        x_now = xs_out[0 : z.xrows, :]
    else:
        data = xs
        x_now = x_old[...]
    obj = data[z.xrows : 2 * z.xrows, :]
    low = data[2 * z.xrows : 3 * z.xrows, :]
    high = data[3 * z.xrows : 4 * z.xrows, :]
    x_new = jnp.minimum(jnp.maximum(x_now - tau * (obj - work[...]), low), high)
    v[...] = 2.0 * x_new - x_now
    v[z.cols :, :] = jnp.where(has_previous, v[z.cols :, :], 0.0)
    move = None
    if ends:
        mean = (x_new + x_now) * (1.0 / INNER)
        moved = mean[0 : z.cols, :] - x_begin[0 : z.cols, :]
        move = total(moved * moved)
        x_out[...] = mean
    else:
        x_out[...] = x_new

    for q in range(-(-z.listed // z.tile)):
        count = min(z.tile, z.listed - q * z.tile)
        chosen = onehot(column_lists(z, halves, q), 0, count, z.cols)
        vectors[q * z.tile : q * z.tile + count, :] = exact_turned_dot(chosen, v[0 : z.cols, :])
    wides = sum(w.shape[0] for w in wide)
    part_rows(vectors[0:wides, :], pairs, 0)
    lane = lax.broadcasted_iota(jnp.int32, (z.tile, z.tile), 1)
    columns = [jnp.zeros((z.tile, z.tile), F32) for _ in range(z.blocks)]
    rows = {}
    for matrix, k in two_units(range(wides), range(wides, z.products)):
        if matrix:
            rows[k] = row_times_tile(z, pairs, k, wide)
            continue
        if k < z.listed:
            tile = tiles[k // z.nt][k % z.nt]
            vector = vectors[k : k + 1, :]
        else:
            tile = halves[k - z.listed][z.link : z.link + z.tile, :]
            vector = v[z.cols + k - z.listed : z.cols + k - z.listed + 1, :]
        column = jnp.sum(tile * vector, axis=1, keepdims=True)
        columns[k // z.tile] = jnp.where(lane == k % z.tile, column, columns[k // z.tile])
    for b in range(z.blocks):
        count = min(z.zrows - b * z.tile, z.tile)
        zmsg[b * z.tile : b * z.tile + count, :] = columns[b].T[0:count, :]
    for k, row_k in rows.items():
        zmsg[k : k + 1, :] = row_k
    if ends:
        zmsg[z.products : z.products + 1, :] = move * jnp.ones((1, z.tile), F32)


def typed(shapes):
    return [s if isinstance(s[0], tuple) else (s, F32) for s in shapes]


def call(z, kernel, operands, shapes, scratch=(), away=0, sems=0, scalar=False, limit=None):
    spaces = [pl.ANY] * away + [pltpu.VMEM] * (len(operands) - away)
    return pl.pallas_call(
        kernel,
        out_shape=[jax.ShapeDtypeStruct(s, kind) for s, kind in typed(shapes)],
        in_specs=[pl.BlockSpec(memory_space=s) for s in spaces],
        out_specs=[
            pl.BlockSpec(memory_space=pltpu.SMEM if scalar else pltpu.VMEM) for _ in shapes
        ],
        scratch_shapes=[pltpu.VMEM(s, kind) for s, kind in typed(scratch)]
        + ([pltpu.SemaphoreType.DMA((sems,))] if sems else []),
        compiler_params=pltpu.CompilerParams(vmem_limit_bytes=limit or z.limit),
    )(*operands)


def per_device(
    primal_start,
    dual_start,
    objective,
    right_side,
    upper_bound,
    column_kind,
    row_kind,
    tile_values,
    tile_rows,
    tile_cols,
    coupling,
):
    tile = tile_values.shape[-1]
    listed = tile_values.shape[3]
    z = Sizes(
        lax.axis_size("period"),
        lax.axis_size("row"),
        lax.axis_size("col"),
        tile,
        listed,
        primal_start.shape[0],
        dual_start.shape[0],
    )
    part = functools.partial
    line = lambda rows: (rows, tile)
    row_list = tile_rows.reshape(1, listed)
    col_list = tile_cols.reshape(1, listed)
    tiles_away = tile_values.reshape(listed, tile, tile)
    tiles = exchange(tiles_away, "row")
    (zmsg,) = call(
        z,
        part(dual_message_kernel, z),
        (dual_start, right_side, row_kind, objective, row_list),
        [line(3 * z.rs + 8)],
        [(line(z.rs), jnp.int32), line(z.cs), ((1, listed), jnp.int32)],
        away=5,
        sems=5,
        limit=AWAY,
    )
    (xmsg,) = call(
        z,
        part(primal_message_kernel, z),
        (
            primal_start,
            objective,
            upper_bound,
            column_kind,
            col_list,
            coupling.reshape(tile, tile),
        ),
        [line(z.link + tile)],
        [line(z.cs), (line(z.cs), jnp.int32), ((1, listed), jnp.int32)],
        away=6,
        sems=6,
        limit=AWAY,
    )
    block = (listed, tile, tile)
    wide_block = (listed, tile, 2 * tile)
    half_block = (listed // 2, tile, 2 * tile)
    own_tiles, wide, token = call(
        z,
        part(fetch_kernel, z),
        (tiles_away,),
        [block, (wide_block, BF16), line(8)],
        away=1,
        sems=FETCHES,
        limit=FETCH,
    )
    slots = exchange(zmsg, "col")
    halves = exchange(xmsg, "row")
    (gathered,) = call(z, part(assemble_kernel, z), [token] + slots[::-1], [line(z.setup)])
    shared = exchange(gathered, "row")

    products = line(up(z.products, 8))
    y, xs, g, msg = call(
        z,
        part(first_kernel, z),
        (*shared, *halves, *tiles[1:], wide),
        [line(z.nr * z.rows), line(4 * z.xrows), line(z.xrows), line(z.hop_first)],
        [products, line(up(3 * listed, 8))],
    )
    turned, sibling_wide, sibling_turned = call(
        z,
        part(turn_kernel, z),
        (g, own_tiles, tiles[1]),
        [(wide_block, BF16), (half_block, BF16), (half_block, BF16)],
    )
    x = None
    weight = None
    y_begin, x_begin = y, None
    for step in range(ROUNDS * INNER):
        starts = step % INNER == 0
        ends = step % INNER == INNER - 1
        first, last = step == 0, step == ROUNDS * INNER - 1
        got = period_exchange(msg, starts)
        operands = ([] if first else [weight]) + [g, msg, *got[::-1], xs]
        operands += ([] if first else [x]) + ([x_begin] if ends else []) + [*halves, *tiles[1:], turned, sibling_turned]
        shapes = [line(z.xrows), line(z.zrows)]
        shapes += ([line(8)] if starts else []) + ([line(4 * z.xrows)] if first else [])
        outs = call(
            z,
            part(primal_kernel, z, starts, first, ends),
            operands,
            shapes,
            [line(z.xrows), line(z.xrows), line(up(z.listed, 8)), line(up(3 * listed, 8))],
        )
        x_next, zmsg = outs[:2]
        if starts:
            weight = outs[2]
        if first:
            xs = outs[3]
            x = xs[0 : z.xrows]
        if starts:
            x_begin = x
        x = x_next
        slots = exchange(zmsg, "col")
        if last:
            break
        order = list(range(z.nc))[::-1]
        if first:
            order = order[-2:-1] + order[:-2] + order[-1:]
        operands = [weight, *[slots[d] for d in order], *shared, *halves, *tiles[1:], wide, sibling_wide, y]
        y_next, g, msg = call(
            z,
            part(dual_kernel, z, ends, order),
            operands + ([y_begin] if ends else []),
            [line(z.nr * z.rows), line(z.xrows), line(z.hop)],
            [products, line(up(3 * listed, 8))],
        )
        y = y_next
        if ends:
            y_begin = y
    y, sums = call(
        z,
        part(last_kernel, z),
        (weight, *slots[::-1], *shared, y, y_begin),
        [line(z.nr * z.rows), line(8)],
        [line(z.nr * z.rows)],
    )
    got = period_exchange(sums, True)
    primal, dual, token = call(
        z, part(output_kernel, z), (x, y), [line(z.cs), line(z.rs), line(8)]
    )
    (final,) = call(
        z,
        part(weight_kernel, z),
        (token, weight, sums, *got[::-1]),
        [(1,)],
        scalar=True,
    )
    return (primal, dual, final.reshape(()))


def solution(mesh):
    in_specs = (
        P(("period", "row"), "col"),
        P(("period", "col"), "row"),
        P(("period", "row"), "col"),
        P(("period", "col"), "row"),
        P(("period", "row"), "col"),
        P(("period", "row"), "col"),
        P(("period", "col"), "row"),
        P("period", "row", "col", None, None, None),
        P("period", "row", "col", None),
        P("period", "row", "col", None),
        P("period", "row", "col", None, None),
    )
    out_specs = (P(("period", "row"), "col"), P(("period", "col"), "row"), P())
    return jax.shard_map(
        per_device, mesh=mesh, in_specs=in_specs, out_specs=out_specs, check_vma=False
    )
```

```python
import functools
import jax
import jax.numpy as jnp
from jax import lax
from jax.experimental import pallas as pl
from jax.experimental.pallas import tpu as pltpu
from jax.sharding import PartitionSpec as P

ROUNDS = 2
INNER = 2
STEP_SCALE = 0.15
EPSILON = 1e-06
F32 = jnp.float32
BF16 = jnp.bfloat16
FETCH = 49 << 20
AWAY = 59 << 20
FETCHES = 8


def up(n, m):
    return -(-n // m) * m


def peer(me, j, n):
    return me ^ j if n & (n - 1) == 0 else lax.rem(me + j, n)


def from_peer(x, axis, j):
    n = lax.axis_size(axis)
    pairs = [((i ^ j) if n & (n - 1) == 0 else (i + j) % n, i) for i in range(n)]
    return lax.ppermute(x, axis, pairs)


def exchange(x, axis):
    return [x] + [from_peer(x, axis, j) for j in range(1, lax.axis_size(axis))]


def period_exchange(x, all_of_them):
    n = lax.axis_size("period")
    if n % 2 == 0 and n > 2:
        even = {i: i ^ 1 for i in range(n)}
        odd = {i: ((i - 1) if i % 2 == 0 else (i + 1)) % n for i in range(n)}
        got = [lax.ppermute(x, "period", [(m[i], i) for i in range(n)]) for m in (even, odd)]
    else:
        got = [lax.ppermute(x, "period", [((i + s) % n, i) for i in range(n)]) for s in (1, n - 1)]
    if all_of_them:
        got += [
            lax.ppermute(x, "period", [((i + s) % n, i) for i in range(n)]) for s in range(2, n - 1)
        ]
    return got


def next_and_previous(first, second, size, me):
    if size % 2 == 0 and size > 2:
        is_even = lax.rem(me, 2) == 0
        return jnp.where(is_even, first, second), jnp.where(is_even, second, first)
    return first, second


def onehot(lists, first, count, height):
    spots = lax.broadcasted_iota(jnp.int32, (height, count), 0).astype(F32)
    return jnp.where(spots == lists[:, first : first + count], 1.0, 0.0).astype(BF16)


def total(x):
    return jnp.sum(jnp.sum(x, axis=0, keepdims=True), axis=1, keepdims=True)


class Sizes:
    def __init__(self, mesh_period, mesh_row, mesh_col, tile, listed, col_share, row_share):
        self.np, self.nr, self.nc = mesh_period, mesh_row, mesh_col
        self.tile, self.nt = tile, listed
        self.cs, self.rs = col_share, row_share
        self.cols, self.rows = col_share * mesh_row, row_share * mesh_col
        self.listed = self.nr * self.nt
        self.products = self.listed + self.nr
        self.blocks = -(-self.products // tile)
        self.zrows = up(self.products + 1, 8)
        self.ghosts = up(self.nr, 8)
        self.xrows = self.cols + self.ghosts
        self.hop = up(2 * self.nr + 2, 8)
        self.hop_first = self.hop + up(4 * self.nr, 8)
        self.group = tile // self.nt
        self.row_lists = -(-self.nc // self.group)
        self.setup = 3 * self.rows + up(self.row_lists + 2, 8)
        self.link = 4 * col_share + 8
        self.limit = (self.nr * listed * tile * tile * 4 * 3) // 2 + (10 << 20)


def copies(pairs, sems):
    started = [pltpu.make_async_copy(src, dst, sems.at[i]) for i, (src, dst) in enumerate(pairs)]
    for copy in started:
        copy.start()
    for copy in started:
        copy.wait()


def dual_message_kernel(z, dual_at, rhs_at, rkind_at, obj_at, rlist_at, zmsg, rkind, obj, rlist, sems):
    rs = z.rs
    copies(
        [
            (dual_at, zmsg.at[0:rs, :]),
            (rhs_at, zmsg.at[rs : 2 * rs, :]),
            (rkind_at, rkind),
            (obj_at, obj),
            (rlist_at, rlist),
        ],
        sems,
    )
    rhs = zmsg[rs : 2 * rs, :]
    zmsg[2 * rs : 3 * rs, :] = jnp.where(rkind[...] == 0, 0.0, -jnp.inf)
    zmsg[3 * rs : 3 * rs + 8, :] = jnp.zeros((8, z.tile), F32)
    zmsg[3 * rs : 3 * rs + 1, 0 : z.nt] = rlist[...].astype(F32)
    ones = jnp.ones((1, z.tile), F32)
    zmsg[3 * rs + 1 : 3 * rs + 2, :] = total(obj[...] * obj[...]) * ones
    zmsg[3 * rs + 2 : 3 * rs + 3, :] = total(rhs * rhs) * ones


def primal_message_kernel(
    z, x_at, obj_at, ub_at, ckind_at, clist_at, link_at, xmsg, ub, ckind, clist, sems
):
    cs = z.cs
    copies(
        [
            (x_at, xmsg.at[0:cs, :]),
            (obj_at, xmsg.at[cs : 2 * cs, :]),
            (ub_at, ub),
            (ckind_at, ckind),
            (clist_at, clist),
            (link_at, xmsg.at[z.link : z.link + z.tile, :]),
        ],
        sems,
    )
    kind = ckind[...]
    xmsg[2 * cs : 3 * cs, :] = jnp.where(kind == 2, -jnp.inf, 0.0)
    xmsg[3 * cs : 4 * cs, :] = jnp.where(kind == 1, ub[...], jnp.inf)
    xmsg[4 * cs : 4 * cs + 8, :] = jnp.zeros((8, z.tile), F32)
    xmsg[4 * cs : 4 * cs + 1, 0 : z.nt] = clist[...].astype(F32)


def two_parts(values):
    head = values.astype(BF16)
    return head, (values - head.astype(F32)).astype(BF16)


def put_parts(wide, values):
    tile = values.shape[-1]
    wide[:, 0:tile], wide[:, tile : 2 * tile] = two_parts(values)


def fetch_kernel(z, tiles_at, tiles, wide, token, sems):
    step = max(z.nt // FETCHES, 1)
    cuts = range(0, z.nt, step)
    started = [
        pltpu.make_async_copy(tiles_at.at[i : i + step], tiles.at[i : i + step], sems.at[c])
        for c, i in enumerate(cuts)
    ]
    for copy in started:
        copy.start()
    token[...] = jnp.zeros_like(token)
    for i, copy in zip(cuts, started):
        copy.wait()
        for n in range(i, i + step):
            put_parts(wide.at[n], tiles[n])


def turn_kernel(z, when, tiles, sibling, turned, sibling_wide, sibling_turned):
    for n in range(z.nt):
        put_parts(turned.at[n], tiles[n].T)
    for n in range(z.nt // 2):
        put_parts(sibling_wide.at[n], sibling[n])
        put_parts(sibling_turned.at[n], sibling[n].T)


def part_rows(values, pairs, first):
    head, rest = two_parts(values)
    count = values.shape[0]
    pairs[pl.ds(2 * first, count, stride=2), :] = head.astype(F32)
    pairs[pl.ds(2 * first + 1, count, stride=2), :] = rest.astype(F32)


def row_times_tile(z, pairs, k, wide):
    row = pairs[2 * k : 2 * k + 2, :].astype(BF16)
    product = jnp.dot(row, wide[k // z.nt][k % z.nt], preferred_element_type=F32)
    head, rest = product[:, 0 : z.tile], product[:, z.tile : 2 * z.tile]
    return head[0:1] + (head[1:2] + rest[0:1])


def two_units(matrix, vector):
    jobs = [((i + 0.5) / len(matrix), 0, k) for i, k in enumerate(matrix)]
    jobs += [((i + 0.5) / len(vector), 1, k) for i, k in enumerate(vector)]
    return [(kind == 0, k) for _, kind, k in sorted(jobs)]


def put_list(z, lists, rows, i):
    lane = lax.broadcasted_iota(jnp.int32, (8, z.tile), 1)
    moved = pltpu.roll(rows, i * z.nt, 1) if i else rows
    return jnp.where(lane // z.nt == i, moved, lists)


def assemble_kernel(z, *refs):
    slots, out = refs[-2:0:-1], refs[-1]
    me = lax.axis_index("col")
    base = 3 * z.rows
    out[base:, :] = jnp.zeros((z.setup - base, z.tile), F32)
    sums = jnp.zeros((2, z.tile), F32)
    lists = [jnp.zeros((8, z.tile), F32) for _ in range(z.row_lists)]
    for d, slot in enumerate(slots):
        at = peer(me, d, z.nc) * z.rs
        for part in range(3):
            spot = pl.ds(pl.multiple_of(part * z.rows + at, z.rs), z.rs)
            out[spot, :] = slot[part * z.rs : (part + 1) * z.rs, :]
        q = d // z.group
        lists[q] = put_list(z, lists[q], slot[3 * z.rs : 3 * z.rs + 8, :], d % z.group)
        sums = sums + slot[3 * z.rs + 1 : 3 * z.rs + 3, :]
    for q in range(z.row_lists):
        out[base + q : base + q + 1, :] = lists[q][0:1, :]
    out[base + z.row_lists : base + z.row_lists + 2, :] = sums


def three_parts(values):
    head = values.astype(BF16)
    rest = values - head.astype(F32)
    middle = rest.astype(BF16)
    return head, middle, (rest - middle.astype(F32)).astype(BF16)


def exact_dot(chosen, values):
    head, middle, tail = three_parts(values)
    dot = functools.partial(jnp.dot, preferred_element_type=F32)
    return dot(chosen, head) + (dot(chosen, middle) + dot(chosen, tail))


def exact_turned_dot(left, right):
    dot = lambda a, b: lax.dot_general(
        a, b, (((0,), (0,)), ((), ())), preferred_element_type=F32
    )
    if left.dtype == BF16:
        head, middle, tail = three_parts(right)
        return dot(left, head) + (dot(left, middle) + dot(left, tail))
    head, middle, tail = three_parts(left)
    return dot(head, right) + (dot(middle, right) + dot(tail, right))


def transposed_products(z, y_at, shared, tiles, wide, links, products, pairs):
    me = lax.axis_index("col")
    columns, on_matrix, on_vector = [], [], []
    for j in range(z.nr):
        lists = shared[j][3 * z.rows : 3 * z.rows + 1, :]
        block = y_at[j * z.rows : (j + 1) * z.rows, :]
        wides = wide[j].shape[0] if j < len(wide) else 0
        columns.append((None, wides))
        if wides:
            chosen = onehot(lists, 0, wides, z.rows)
            part_rows(exact_turned_dot(chosen, block), pairs, j * z.nt)
        if wides < z.nt:
            chosen = onehot(lists, wides, z.nt - wides, z.rows)
            columns[j] = (exact_turned_dot(block, chosen), wides)
        on_matrix += range(j * z.nt, j * z.nt + wides)
        on_vector += range(j * z.nt + wides, (j + 1) * z.nt)
    for matrix, k in two_units(on_matrix, on_vector):
        j, n = k // z.nt, k % z.nt
        if matrix:
            products[k : k + 1, :] = row_times_tile(z, pairs, k, wide)
        else:
            block, skip = columns[j]
            column = block[:, n - skip : n - skip + 1]
            products[k : k + 1, :] = jnp.sum(tiles[j][n] * column, axis=0, keepdims=True)
    for j in range(z.nr):
        first = y_at[pl.ds(j * z.rows + me * z.rs, 1), :]
        coupled = jnp.broadcast_to(first, (8, z.tile)).T
        k = z.listed + j
        link = links[j][z.link : z.link + z.tile, :]
        products[k : k + 1, :] = jnp.sum(link * coupled[:, 0:1], axis=0, keepdims=True)


def column_lists(z, halves, q):
    lists = jnp.zeros((8, z.tile), F32)
    for i in range(min(z.group, z.nr - q * z.group)):
        at = 4 * z.cs
        lists = put_list(z, lists, halves[q * z.group + i][at : at + 8, :], i)
    return lists[0:1, :]


def gradient_part(z, products, halves, g, msg, sums):
    row = lax.axis_index("row")
    full = jnp.zeros((z.cols, z.tile), F32)
    for q in range(-(-z.listed // z.tile)):
        count = min(z.tile, z.listed - q * z.tile)
        chosen = onehot(column_lists(z, halves, q), 0, count, z.cols)
        full = full + exact_dot(chosen, products[q * z.tile : q * z.tile + count, :])
    g[0 : z.cols, :] = full
    g[z.cols :, :] = jnp.zeros((z.ghosts, z.tile), F32)
    msg[...] = jnp.zeros_like(msg)
    for j in range(z.nr):
        outflow = products[z.listed + j : z.listed + j + 1, :]
        g[z.cols + j : z.cols + j + 1, :] = outflow
        msg[j : j + 1, :] = outflow
        last = peer(row, j, z.nr) * z.cs + z.cs - 1
        msg[z.nr + j : z.nr + j + 1, :] = g[pl.ds(last, 1), :]
    for i, value in enumerate(sums):
        msg[2 * z.nr + i : 2 * z.nr + i + 1, :] = value


def first_kernel(z, *refs):
    shared, refs = refs[: z.nr], refs[z.nr :]
    halves, refs = refs[: z.nr], refs[z.nr :]
    tiles, refs = (None, *refs[: z.nr - 1]), refs[z.nr - 1 :]
    wide, refs = refs[:1], refs[1:]
    y, xs, g, msg, products, pairs = refs
    row = lax.axis_index("row")
    for j in range(z.nr):
        y[j * z.rows : (j + 1) * z.rows, :] = shared[j][0 : z.rows, :]
        at = peer(row, j, z.nr) * z.cs
        for part in range(4):
            spot = pl.ds(pl.multiple_of(part * z.xrows + at, 8), z.cs)
            xs[spot, :] = halves[j][part * z.cs : (part + 1) * z.cs, :]
    transposed_products(z, y, shared, tiles, wide, halves, products, pairs)
    base = 3 * z.rows + z.row_lists
    sums = [sum(s[base + i : base + i + 1, :] for s in shared) for i in range(2)]
    gradient_part(z, products, halves, g, msg, sums)
    for part in range(4):
        xs[part * z.xrows + z.cols : (part + 1) * z.xrows, :] = jnp.zeros((z.ghosts, z.tile), F32)
        for j in range(z.nr):
            to = z.hop + part * z.nr + j
            msg[to : to + 1, :] = halves[j][(part + 1) * z.cs - 1 : (part + 1) * z.cs, :]


def dual_part(z, w, slots, shared, y_old, y_out):
    me = lax.axis_index("col")
    sigma = STEP_SCALE * w[0:1, :]
    spots = lax.broadcasted_iota(jnp.int32, (z.rows, z.tile), 0)
    for j in range(z.nr):
        summed = jnp.zeros((z.rows, z.tile), F32)
        for q in range(z.row_lists):
            ds = range(q * z.group, min((q + 1) * z.group, z.nc))
            lists = shared[j][3 * z.rows + q : 3 * z.rows + q + 1, :]
            chosen = onehot(lists, 0, len(ds) * z.nt, z.rows)
            parts = [slots[d][j * z.nt : (j + 1) * z.nt, :] for d in ds]
            summed = summed + exact_dot(chosen, jnp.concatenate(parts, axis=0))
        for d in range(z.nc):
            inflow = slots[d][z.listed + j : z.listed + j + 1, :]
            summed = summed + jnp.where(spots == peer(me, d, z.nc) * z.rs, inflow, 0.0)
        spot = slice(j * z.rows, (j + 1) * z.rows)
        moved = y_old[spot, :] + sigma * (shared[j][z.rows : 2 * z.rows, :] - summed)
        y_out[spot, :] = jnp.maximum(moved, shared[j][2 * z.rows : 3 * z.rows, :])


def mean_and_move(now, before, begin):
    mean = (now + before) * (1.0 / INNER)
    return mean, total((mean - begin) * (mean - begin))


def dual_kernel(z, ends, order, *refs):
    w, refs = refs[0], refs[1:]
    slots, refs = [refs[order.index(d)] for d in range(z.nc)], refs[z.nc :]
    shared, refs = refs[: z.nr], refs[z.nr :]
    halves, refs = refs[: z.nr], refs[z.nr :]
    tiles, refs = (None, *refs[: z.nr - 1]), refs[z.nr - 1 :]
    wide, refs = refs[:2], refs[2:]
    y_old = refs[0]
    y_begin = refs[1] if ends else None
    y_out, g, msg, products, pairs = refs[-5:]
    dual_part(z, w, slots, shared, y_old, y_out)
    sums = []
    if ends:
        mean, move = mean_and_move(y_out[...], y_old[...], y_begin[...])
        y_out[...] = mean
        moved = sum(s[z.products : z.products + 1, :] for s in slots)
        sums = [moved, move * jnp.ones((1, z.tile), F32)]
    transposed_products(z, y_out, shared, tiles, wide, halves, products, pairs)
    gradient_part(z, products, halves, g, msg, sums)


def last_kernel(z, *refs):
    w, refs = refs[0], refs[1:]
    slots, refs = refs[: z.nc][::-1], refs[z.nc :]
    shared, refs = refs[: z.nr], refs[z.nr :]
    y_old, y_begin, y_mean, msg, y_new = refs
    dual_part(z, w, slots, shared, y_old, y_new)
    mean, move = mean_and_move(y_new[...], y_old[...], y_begin[...])
    y_mean[...] = mean
    msg[...] = jnp.zeros_like(msg)
    msg[0:1, :] = sum(s[z.products : z.products + 1, :] for s in slots)
    msg[1:2, :] = move * jnp.ones((1, z.tile), F32)


def output_kernel(z, x, y, x_out, y_out, token):
    row, col = lax.axis_index("row"), lax.axis_index("col")
    x_out[...] = x[pl.ds(pl.multiple_of(row * z.cs, z.cs), z.cs), :]
    y_out[...] = y[pl.ds(pl.multiple_of(col * z.rs, z.rs), z.rs), :]
    token[...] = jnp.zeros_like(token)


def weight_kernel(z, *refs):
    w, msgs, out = refs[1], refs[2:-1], refs[-1]
    dx = sum(m[0:1, :] for m in msgs)
    dy = sum(m[1:2, :] for m in msgs)
    new = jnp.sqrt(w[0:1, :] * jnp.sqrt((dx + EPSILON) / (dy + EPSILON)))
    out[0] = new[0, 0]


def primal_kernel(z, starts, first, ends, *refs):
    w_old, refs = (None, refs) if first else (refs[0], refs[1:])
    g, own, refs = refs[0], refs[1], refs[2:]
    count = (z.np - 1) if starts else 2
    got, refs = refs[:count][::-1], refs[count:]
    xs, refs = refs[0], refs[1:]
    x_old, refs = (None, refs) if first else (refs[0], refs[1:])
    x_begin, refs = (refs[0], refs[1:]) if ends else (None, refs)
    halves, refs = refs[: z.nr], refs[z.nr :]
    tiles, refs = (None, *refs[: z.nr - 1]), refs[z.nr - 1 :]
    wide, refs = refs[:2], refs[2:]
    x_out, zmsg, refs = refs[0], refs[1], refs[2:]
    w_out, refs = (refs[0], refs[1:]) if starts else (None, refs)
    xs_out, refs = (refs[0], refs[1:]) if first else (None, refs)
    work, v, vectors, pairs = refs
    period, row = lax.axis_index("period"), lax.axis_index("row")

    if starts:
        s1 = own[2 * z.nr : 2 * z.nr + 1, :]
        s2 = own[2 * z.nr + 1 : 2 * z.nr + 2, :]
        for m in got:
            s1 = s1 + m[2 * z.nr : 2 * z.nr + 1, :]
            s2 = s2 + m[2 * z.nr + 1 : 2 * z.nr + 2, :]
        ratio = (s1 + EPSILON) / (s2 + EPSILON)
        weight = jnp.sqrt(ratio) if first else jnp.sqrt(w_old[0:1, :] * jnp.sqrt(ratio))
        w_out[...] = jnp.broadcast_to(weight, w_out.shape)
    else:
        weight = w_old[0:1, :]
    tau = STEP_SCALE / weight

    after, before = next_and_previous(got[0][...], got[1][...], z.np, period)
    has_next = period < z.np - 1
    has_previous = period > 0
    work[...] = g[...]
    for j in range(z.nr):
        last_row = pl.ds(peer(row, j, z.nr) * z.cs + z.cs - 1, 1)
        outflow = jnp.where(has_next, after[j : j + 1, :], 0.0)
        work[last_row, :] = work[last_row, :] + outflow
        ghost = slice(z.cols + j, z.cols + j + 1)
        work[ghost, :] = work[ghost, :] + before[z.nr + j : z.nr + j + 1, :]
    if first:
        xs_out[...] = xs[...]
        for part in range(4):
            for j in range(z.nr):
                to = part * z.xrows + z.cols + j
                at = z.hop + part * z.nr + j
                xs_out[to : to + 1, :] = before[at : at + 1, :]
        data = xs_out
        x_now = xs_out[0 : z.xrows, :]
    else:
        data = xs
        x_now = x_old[...]
    obj = data[z.xrows : 2 * z.xrows, :]
    low = data[2 * z.xrows : 3 * z.xrows, :]
    high = data[3 * z.xrows : 4 * z.xrows, :]
    x_new = jnp.minimum(jnp.maximum(x_now - tau * (obj - work[...]), low), high)
    v[...] = 2.0 * x_new - x_now
    v[z.cols :, :] = jnp.where(has_previous, v[z.cols :, :], 0.0)
    move = None
    if ends:
        mean = (x_new + x_now) * (1.0 / INNER)
        moved = mean[0 : z.cols, :] - x_begin[0 : z.cols, :]
        move = total(moved * moved)
        x_out[...] = mean
    else:
        x_out[...] = x_new

    for q in range(-(-z.listed // z.tile)):
        count = min(z.tile, z.listed - q * z.tile)
        chosen = onehot(column_lists(z, halves, q), 0, count, z.cols)
        vectors[q * z.tile : q * z.tile + count, :] = exact_turned_dot(chosen, v[0 : z.cols, :])
    wides = sum(w.shape[0] for w in wide)
    part_rows(vectors[0:wides, :], pairs, 0)
    lane = lax.broadcasted_iota(jnp.int32, (z.tile, z.tile), 1)
    columns = [jnp.zeros((z.tile, z.tile), F32) for _ in range(z.blocks)]
    rows = {}
    for matrix, k in two_units(range(wides), range(wides, z.products)):
        if matrix:
            rows[k] = row_times_tile(z, pairs, k, wide)
            continue
        if k < z.listed:
            tile = tiles[k // z.nt][k % z.nt]
            vector = vectors[k : k + 1, :]
        else:
            tile = halves[k - z.listed][z.link : z.link + z.tile, :]
            vector = v[z.cols + k - z.listed : z.cols + k - z.listed + 1, :]
        column = jnp.sum(tile * vector, axis=1, keepdims=True)
        columns[k // z.tile] = jnp.where(lane == k % z.tile, column, columns[k // z.tile])
    for b in range(z.blocks):
        count = min(z.zrows - b * z.tile, z.tile)
        zmsg[b * z.tile : b * z.tile + count, :] = columns[b].T[0:count, :]
    for k, row_k in rows.items():
        zmsg[k : k + 1, :] = row_k
    if ends:
        zmsg[z.products : z.products + 1, :] = move * jnp.ones((1, z.tile), F32)


def typed(shapes):
    return [s if isinstance(s[0], tuple) else (s, F32) for s in shapes]


def call(z, kernel, operands, shapes, scratch=(), away=0, sems=0, scalar=False, limit=None):
    spaces = [pl.ANY] * away + [pltpu.VMEM] * (len(operands) - away)
    return pl.pallas_call(
        kernel,
        out_shape=[jax.ShapeDtypeStruct(s, kind) for s, kind in typed(shapes)],
        in_specs=[pl.BlockSpec(memory_space=s) for s in spaces],
        out_specs=[
            pl.BlockSpec(memory_space=pltpu.SMEM if scalar else pltpu.VMEM) for _ in shapes
        ],
        scratch_shapes=[pltpu.VMEM(s, kind) for s, kind in typed(scratch)]
        + ([pltpu.SemaphoreType.DMA((sems,))] if sems else []),
        compiler_params=pltpu.CompilerParams(vmem_limit_bytes=limit or z.limit),
    )(*operands)


def per_device(
    primal_start,
    dual_start,
    objective,
    right_side,
    upper_bound,
    column_kind,
    row_kind,
    tile_values,
    tile_rows,
    tile_cols,
    coupling,
):
    tile = tile_values.shape[-1]
    listed = tile_values.shape[3]
    z = Sizes(
        lax.axis_size("period"),
        lax.axis_size("row"),
        lax.axis_size("col"),
        tile,
        listed,
        primal_start.shape[0],
        dual_start.shape[0],
    )
    part = functools.partial
    line = lambda rows: (rows, tile)
    row_list = tile_rows.reshape(1, listed)
    col_list = tile_cols.reshape(1, listed)
    tiles_away = tile_values.reshape(listed, tile, tile)
    tiles = exchange(tiles_away, "row")
    (zmsg,) = call(
        z,
        part(dual_message_kernel, z),
        (dual_start, right_side, row_kind, objective, row_list),
        [line(3 * z.rs + 8)],
        [(line(z.rs), jnp.int32), line(z.cs), ((1, listed), jnp.int32)],
        away=5,
        sems=5,
        limit=AWAY,
    )
    (xmsg,) = call(
        z,
        part(primal_message_kernel, z),
        (
            primal_start,
            objective,
            upper_bound,
            column_kind,
            col_list,
            coupling.reshape(tile, tile),
        ),
        [line(z.link + tile)],
        [line(z.cs), (line(z.cs), jnp.int32), ((1, listed), jnp.int32)],
        away=6,
        sems=6,
        limit=AWAY,
    )
    block = (listed, tile, tile)
    wide_block = (listed, tile, 2 * tile)
    half_block = (listed // 2, tile, 2 * tile)
    own_tiles, wide, token = call(
        z,
        part(fetch_kernel, z),
        (tiles_away,),
        [block, (wide_block, BF16), line(8)],
        away=1,
        sems=FETCHES,
        limit=FETCH,
    )
    slots = exchange(zmsg, "col")
    halves = exchange(xmsg, "row")
    (gathered,) = call(z, part(assemble_kernel, z), [token] + slots[::-1], [line(z.setup)])
    shared = exchange(gathered, "row")

    products = line(up(z.products, 8))
    y, xs, g, msg = call(
        z,
        part(first_kernel, z),
        (*shared, *halves, *tiles[1:], wide),
        [line(z.nr * z.rows), line(4 * z.xrows), line(z.xrows), line(z.hop_first)],
        [products, line(up(3 * listed, 8) + 8)],
    )
    turned, sibling_wide, sibling_turned = call(
        z,
        part(turn_kernel, z),
        (g, own_tiles, tiles[1]),
        [(wide_block, BF16), (half_block, BF16), (half_block, BF16)],
    )
    x = None
    weight = None
    y_begin, x_begin = y, None
    for step in range(ROUNDS * INNER):
        starts = step % INNER == 0
        ends = step % INNER == INNER - 1
        first, last = step == 0, step == ROUNDS * INNER - 1
        got = period_exchange(msg, starts)
        operands = ([] if first else [weight]) + [g, msg, *got[::-1], xs]
        operands += ([] if first else [x]) + ([x_begin] if ends else []) + [*halves, *tiles[1:], turned, sibling_turned]
        shapes = [line(z.xrows), line(z.zrows)]
        shapes += ([line(8)] if starts else []) + ([line(4 * z.xrows)] if first else [])
        outs = call(
            z,
            part(primal_kernel, z, starts, first, ends),
            operands,
            shapes,
            [line(z.xrows), line(z.xrows), line(up(z.listed, 8)), line(up(3 * listed, 8) + 8)],
        )
        x_next, zmsg = outs[:2]
        if starts:
            weight = outs[2]
        if first:
            xs = outs[3]
            x = xs[0 : z.xrows]
        if starts:
            x_begin = x
        x = x_next
        slots = exchange(zmsg, "col")
        if last:
            break
        order = list(range(z.nc))[::-1]
        if first:
            order = order[-2:-1] + order[:-2] + order[-1:]
        operands = [weight, *[slots[d] for d in order], *shared, *halves, *tiles[1:], wide, sibling_wide, y]
        y_next, g, msg = call(
            z,
            part(dual_kernel, z, ends, order),
            operands + ([y_begin] if ends else []),
            [line(z.nr * z.rows), line(z.xrows), line(z.hop)],
            [products, line(up(3 * listed, 8) + 8)],
        )
        y = y_next
        if ends:
            y_begin = y
    y, sums = call(
        z,
        part(last_kernel, z),
        (weight, *slots[::-1], *shared, y, y_begin),
        [line(z.nr * z.rows), line(8)],
        [line(z.nr * z.rows)],
    )
    got = period_exchange(sums, True)
    primal, dual, token = call(
        z, part(output_kernel, z), (x, y), [line(z.cs), line(z.rs), line(8)]
    )
    (final,) = call(
        z,
        part(weight_kernel, z),
        (token, weight, sums, *got[::-1]),
        [(1,)],
        scalar=True,
    )
    return (primal, dual, final.reshape(()))


def solution(mesh):
    in_specs = (
        P(("period", "row"), "col"),
        P(("period", "col"), "row"),
        P(("period", "row"), "col"),
        P(("period", "col"), "row"),
        P(("period", "row"), "col"),
        P(("period", "row"), "col"),
        P(("period", "col"), "row"),
        P("period", "row", "col", None, None, None),
        P("period", "row", "col", None),
        P("period", "row", "col", None),
        P("period", "row", "col", None, None),
    )
    out_specs = (P(("period", "row"), "col"), P(("period", "col"), "row"), P())
    return jax.shard_map(
        per_device, mesh=mesh, in_specs=in_specs, out_specs=out_specs, check_vma=False
    )
```
